768 devices in a mesh: tok: 64 (over z_lo, y, core), fin: 4 (over x), fout: 3 (over z_hi).
Axes of the slice: x: 4, y: 8, z: 12 (z_hi: 3, z_lo: 4; z = z_hi * 4 + z_lo), core: 2. Of those that a mesh axis runs over, the one named last changes fastest.
Arguments:
- tokens: bfloat16 [384, 6144], P('tok', 'fin'), may hold values from -6 to 6
- cotangent: bfloat16 [384, 6144], P('tok', 'fin'), may hold values from -6 to 6
- image_lengths: int32 [16], replicated, may hold values from 1 to 48, 336 in all
- fc1_weight: bfloat16 [6144, 24576], P('fin', ('tok', 'fout')), may hold values from -0.078125 to 0.078125
- fc2_weight: bfloat16 [24576, 6144], P(('tok', 'fout'), 'fin'), may hold values from -0.0390625 to 0.0390625
Outputs:
- block_out: bfloat16 [384, 6144], P('tok', 'fin')
- grad_tokens: bfloat16 [384, 6144], P('tok', 'fin')
- grad_fc1: float32 [6144, 24576], P('fin', ('tok', 'fout'))
- grad_fc2: float32 [24576, 6144], P(('tok', 'fout'), 'fin')
The draws below stay inside these ranges and needn't reach their ends.
Inputs may be any that keep to these rules, and one draw needn't show every extreme that they name: `image_lengths`: the spans together cover 7 * 48 rows; the rest are padding rows. Some image has exactly 48 patches.
All inputs are finite; a program needn't handle non-finite values.
Results may differ from the reference program's by a relative error of at most 0.012.
Values may be sent and summed in bfloat16 or wider, within the bound.
A program may use at most 32 MiB of HBM per device.

```python
import math
import jax
import jax.numpy as jnp
import numpy as np
from jax import lax

D = 6144
FF = 24576
IMAGES = 16
TOKENS = 384
MOST = 48


def block_levels(stream_key, extent, pieces, least, largest):
    factor_of, own = 1.0, jax.random.fold_in(stream_key, 6)
    for dim, parts in pieces:
        draws = jnp.exp(jax.random.uniform(jax.random.fold_in(own, dim), (parts,), jnp.float32, least / len(pieces), largest / len(pieces)))
        factor_of = factor_of * jnp.repeat(draws, extent[dim] // parts).reshape([-1 if axis == dim else 1 for axis in range(len(extent))])
    return factor_of


def profile(count, total, reach, skew):
    portions = [(1 << 20) // math.isqrt(standing ** skew) + 1 for standing in range(2, count + 1)]
    rest, holding = total - reach - (count - 1), [1] * (count - 1)
    while rest > 0:
        free = [i for i in range(count - 1) if holding[i] < reach]
        whole, remaining = sum([portions[i] for i in free]), rest
        for i in free:
            extra = min(reach - holding[i], max(1, remaining * portions[i] // whole), rest)
            holding[i] = holding[i] + extra
            rest = rest - extra
    return np.array([reach] + holding)


def ragged(stream_key, amount, total, reach, skew):
    if amount == 2:
        one = jax.random.randint(stream_key, (), max(1, total - reach), min(reach, total - 1) + 1)
        return jnp.stack([one, total - one])
    tallies = jnp.asarray(profile(amount, total, reach, skew), jnp.int32)
    couples = (amount - 1) // 2
    source_of, taker = tallies[1:1 + 2 * couples:2], tallies[2:2 + 2 * couples:2]
    slack = jnp.minimum(source_of - 1, reach - taker)
    passed = jax.random.randint(jax.random.fold_in(stream_key, 1), (couples,), 0, 1 << 20) % (slack + 1)
    tallies = tallies.at[1:1 + 2 * couples:2].set(source_of - passed).at[2:2 + 2 * couples:2].set(taker + passed)
    return tallies[jax.random.permutation(jax.random.fold_in(stream_key, 2), amount)]


def scatter_about(own_key, extent, width, limit, pieces=(), kind=jnp.bfloat16):
    array = jax.random.normal(own_key, extent, jnp.float32) * width
    if len(pieces) > 0:
        array = block_levels(own_key, extent, pieces, -0.22, 0.18) * array
    return jnp.clip(array, min=-limit, max=limit).astype(kind)


def setup_inputs(seed: int = 0) -> dict:
    keys = jax.random.split(jax.random.key(seed), 6)
    return {
        "tokens": scatter_about(keys[0], (TOKENS, D), 1.0, 6.0, ((0, 64), (1, 4))),
        "cotangent": scatter_about(keys[1], (TOKENS, D), 1.0, 6.0, ((0, 64), (1, 4))),
        "image_lengths": ragged(keys[2], IMAGES, TOKENS * 7 // 8, MOST, 2).astype(jnp.int32),
        "fc1_weight": scatter_about(keys[3], (D, FF), D ** -0.5, 0.078125, ((0, 4), (1, 192))),
        "fc2_weight": scatter_about(keys[4], (FF, D), FF ** -0.5, 0.0390625, ((0, 192), (1, 4))),
    }


inv_root_two = 0.7071067811865476
inv_root_two_pi = 0.3989422804014327

def row_weights(lengths, first_row, row_count, longest):
    span_ends = jnp.cumsum(lengths, dtype=jnp.int32)
    starts = span_ends - lengths
    position = first_row + jnp.arange(row_count, dtype=jnp.int32)
    inside = (position[:, None] >= starts[None, :]) & (position[:, None] < span_ends[None, :])
    span_len = lax.optimization_barrier(jnp.sum(jnp.where(inside, lengths[None, :], 0), axis=1))
    is_valid = jnp.any(inside, axis=1)
    length_ratio = jnp.float32(longest) / jnp.maximum(span_len, 1).astype(jnp.float32)
    return jnp.where(is_valid, jnp.sqrt(length_ratio), jnp.float32(0.0))

def activations(preact, grad_act):
    normal_cdf = 0.5 * (1.0 + lax.erf(preact * inv_root_two))
    density = jnp.exp(-0.5 * preact * preact) * inv_root_two_pi
    activated = (preact * normal_cdf).astype(jnp.bfloat16)
    grad_pre = (grad_act * (normal_cdf + preact * density)).astype(jnp.bfloat16)
    return (activated, grad_pre)

def reference(tokens, cotangent, image_lengths, fc1_weight, fc2_weight):
    scaling = row_weights(image_lengths, 0, TOKENS, TOKENS // 8)
    scaled = (cotangent.astype(jnp.float32) * scaling[:, None]).astype(jnp.bfloat16)
    preact = jnp.dot(tokens, fc1_weight, preferred_element_type=jnp.float32)
    grad_act = jnp.dot(scaled, fc2_weight.T, preferred_element_type=jnp.float32)
    activated, grad_pre = activations(preact, grad_act)
    block_out = jnp.dot(activated, fc2_weight, preferred_element_type=jnp.float32).astype(jnp.bfloat16)
    grad_tokens = jnp.dot(grad_pre, fc1_weight.T, preferred_element_type=jnp.float32).astype(jnp.bfloat16)
    grad_fc1 = jnp.dot(tokens.T, grad_pre, preferred_element_type=jnp.float32)
    grad_fc2 = jnp.dot(activated.T, scaled, preferred_element_type=jnp.float32)
    return (block_out, grad_tokens, grad_fc1, grad_fc2)
```

```python
import jax
import jax.numpy as jnp
from jax import lax
from jax.experimental import pallas as pl
from jax.experimental.pallas import tpu as pltpu
from jax.sharding import PartitionSpec as P

inv_root_two = 0.7071067811865476
inv_root_two_pi = 0.3989422804014327

NX, NY, NL, NH = 4, 8, 4, 3
NZ = NL * NH
ROWS = 6
BLOCK = 16
FEAT = 1536
HID = 128
LONGEST = 48
CA, CB = 256, 512
A0, A1 = 0, 2 * CA
N_SEMS = 80

bf16, f32 = jnp.bfloat16, jnp.float32


def kernel(
    tok_ref, cot_ref, len_ref, w1_ref, w2_ref,
    out_ref, gtok_ref, g1_ref, g2_ref,
    xb, xa, xbb, xsa, xsb, wc, wt,
    rs, rr, rown, ag, ags,
    ya, yb, ras, rar, rzs, rz, rz2,
    rbs, rbr, rys, ry, vha, vhb,
    mt, g1v, g2v,
    send_sem, recv_sem, local_sem,
):
    t = lax.axis_index("tok")
    x = lax.axis_index("fin")
    f = lax.axis_index("fout")
    c = lax.rem(t, 2)
    y = lax.rem(lax.div(t, 2), NY)
    zl = lax.div(t, 2 * NY)
    z = f * NL + zl

    def on_y(d):
        return {"tok": (zl * NY + lax.rem(y + d + NY, NY)) * 2 + c}

    def on_z(d):
        far = lax.rem(z + d + NZ, NZ)
        return {
            "tok": (lax.rem(far, NL) * NY + y) * 2 + c,
            "fout": lax.div(far, NL),
        }

    def on_x(d):
        return {"fin": lax.rem(x + d, NX)}

    sibling = {"tok": t + 1 - 2 * c}

    def cls(d):
        return lax.rem(zl + d + NL, NL)

    def row(d):
        return lax.rem(y + d + NY, NY)

    sent = []

    def send(src, dst, device):
        i = len(sent)
        copy = pltpu.make_async_remote_copy(
            src_ref=src, dst_ref=dst,
            send_sem=send_sem.at[i], recv_sem=recv_sem.at[i],
            device_id=device, device_id_type=pl.DeviceIdType.MESH,
        )
        copy.start()
        sent.append(copy)
        return copy

    own_w1 = pltpu.make_async_copy(w1_ref, wc.at[:, 0:HID], local_sem.at[0])
    own_w2 = pltpu.make_async_copy(w2_ref, wt.at[0, 0:HID], local_sem.at[1])
    own_w1.start()
    own_w2.start()

    barrier = pltpu.get_barrier_semaphore()
    partners = (
        [sibling]
        + [on_x(d) for d in (1, 2, 3)]
        + [on_y(d) for d in (1, 2, 3, 4, 5, 6, 7)]
        + [on_z(d) for d in (1, -1, 2, -2, 4, -4)]
    )
    for device in partners:
        pl.semaphore_signal(
            barrier, inc=1, device_id=device, device_id_type=pl.DeviceIdType.MESH
        )

    position = t * ROWS + lax.broadcasted_iota(jnp.int32, (8, 128), 0)
    span = jnp.zeros((8, 128), jnp.int32)
    start = jnp.int32(0)
    for i in range(16):
        length = len_ref[i]
        end = start + length
        span = jnp.where((position >= start) & (position < end), length, span)
        start = end
    ratio = f32(LONGEST) / jnp.maximum(span, 1).astype(f32)
    scale = jnp.where(span > 0, jnp.sqrt(ratio), f32(0.0))
    scale = jnp.concatenate([scale] * (FEAT // 128), axis=1)[0:ROWS]
    xb[...] = jnp.zeros_like(xb)
    xb[0:ROWS] = tok_ref[...].astype(f32)
    xb[8 : 8 + ROWS] = cot_ref[...].astype(f32) * scale
    for s in range(2):
        xa[s, y, zl] = xb[:, A0 + s * CA : A0 + (s + 1) * CA].astype(bf16)
        xbb[s, y, zl] = xb[:, A1 + s * CB : A1 + (s + 1) * CB].astype(bf16)

    pl.semaphore_wait(barrier, len(partners))

    ga_z = []
    gb_y = []
    own_a, own_b = xa.at[:, y, zl], xbb.at[:, y, zl]
    for d in (4, 3, 5, 2, 6, 1, 7):
        gb_y.append(send(own_b, own_b, on_y(d)))
    for d in (1, -1):
        ga_z.append(send(own_a, own_a, on_z(d)))
    for s, d in ((0, 2), (1, -2)):
        ga_z.append(send(xa.at[s, y, zl], xa.at[s, y, zl], on_z(d)))
    sib_w1 = send(w1_ref, wc.at[:, HID : 2 * HID], sibling)
    sib_w2 = send(w2_ref, wt.at[0, HID : 2 * HID], sibling)

    own_w1.wait()
    own_w2.wait()
    wc[:, 2 * HID : 3 * HID] = wt[0, 0:HID].T
    wt[1, 0:HID] = wc[:, 0:HID].T

    def ring_steps(way, s):
        return 4 if way == s else 3

    def gather_y(k, way, s):
        sign = 1 if way == 0 else -1
        part = xa.at[s, row(-sign * k)]
        return send(part, part, on_y(sign))

    for copy in ga_z:
        copy.wait_recv()
    ga_y = {}
    for s in range(2):
        for way in range(2):
            ga_y[way, s] = gather_y(0, way, s)

    for copy in gb_y:
        copy.wait_recv()
    gb_z = {}
    for s, d in ((0, 1), (1, -1), (1, 1), (0, -1)):
        part = xbb.at[s, :, zl]
        gb_z[d, s] = send(part, part, on_z(d))

    def ga_step(k):
        for s in range(2):
            for way in range(2):
                if k < ring_steps(way, s):
                    ga_y[way, s].wait_recv()
                    ga_y[way, s] = gather_y(k, way, s)

    ga_step(1)
    sib_w1.wait_recv()
    sib_w2.wait_recv()
    wc[:, 3 * HID : 4 * HID] = wt[0, HID : 2 * HID].T
    wt[1, HID : 2 * HID] = wc[:, HID : 2 * HID].T
    ga_step(2)
    gb_last = []
    for s, d in ((0, 1), (1, -1)):
        gb_z[d, s].wait_recv()
        part = xbb.at[s, :, cls(-d)]
        gb_last.append(send(part, part, on_z(d)))
    ga_step(3)
    for s in range(2):
        for way in range(2):
            ga_y[way, s].wait_recv()
    gb_z[1, 1].wait_recv()
    gb_z[-1, 0].wait_recv()
    for copy in gb_last:
        copy.wait_recv()

    def partial(q):
        rows = pl.ds(2 * q, 2)
        lhs = jnp.concatenate(
            [xa[s, rows].reshape(128, CA) for s in range(2)]
            + [xbb[s, rows].reshape(128, CB) for s in range(2)],
            axis=1,
        )
        pre = jnp.dot(lhs, wc[:, 0 : 2 * HID], preferred_element_type=f32)
        back = jnp.dot(lhs, wc[:, 2 * HID : 4 * HID], preferred_element_type=f32)
        pre = pre.reshape(8, 2, 8, 2 * HID)[:, 0].reshape(2, 32, 2 * HID)
        back = back.reshape(8, 2, 8, 2 * HID)[:, 1].reshape(2, 32, 2 * HID)
        return jnp.concatenate([pre, back], axis=2)

    x_in = []
    for j, d in enumerate((2, 1, 3)):
        rs[j] = partial(lax.rem(x + d, NX)).astype(bf16)
        x_in.append(send(rs.at[j], rr.at[j], on_x(d)))
    rown[...] = partial(x)
    xs = [send(xa, xsa, sibling), send(xbb, xsb, sibling)]
    for copy in x_in:
        copy.wait_recv()
    total = rown[...]
    for j in range(3):
        total = total + rr[j].astype(f32)
    pre, back = total[:, :, 0 : 2 * HID], total[:, :, 2 * HID : 4 * HID]
    cdf = 0.5 * (1.0 + lax.erf(pre * inv_root_two))
    density = jnp.exp(-0.5 * pre * pre) * inv_root_two_pi
    act = (pre * cdf).astype(bf16)
    gp = (back * (cdf + pre * density)).astype(bf16)
    mine = pl.ds(2 * x, 2)
    for j in range(2):
        lanes = slice(j * HID, (j + 1) * HID)
        ag[mine, j] = jnp.concatenate([act[:, :, lanes], gp[:, :, lanes]], axis=2)
    x_out = [send(ag.at[mine], ag.at[mine], on_x(d)) for d in (2, 1, 3)]
    for copy in x_out:
        copy.wait_recv()
    ag_sib = send(ag.at[:, 1], ags, sibling)

    own = ag[:, 0].reshape(256, 2 * HID)
    sib = ag[:, 1].reshape(256, 2 * HID)
    act2 = jnp.concatenate([own[:, 0:HID], sib[:, 0:HID]], axis=1)
    gp2 = jnp.concatenate([own[:, HID:], sib[:, HID:]], axis=1)

    def outputs(dst, s, width, first):
        for n in range(width // 256):
            cols = slice(first + n * 256, first + (n + 1) * 256)
            to = slice(n * 256, (n + 1) * 256)
            fwd = jnp.dot(act2, wt[0, :, cols], preferred_element_type=f32)
            dst[s, :, :, 0:8, to] = fwd.reshape(NY, NL, 8, 256)
            bwd = jnp.dot(gp2, wt[1, :, cols], preferred_element_type=f32)
            dst[s, :, :, 8:16, to] = bwd.reshape(NY, NL, 8, 256)

    for s in range(2):
        outputs(yb, s, CB, A1 + s * CB)
    rb = {}
    for w, (s, d) in enumerate(((0, 1), (1, -1))):
        rbs[w] = yb[s, :, cls(2)].astype(bf16)
        rb[0, w] = send(rbs.at[w], rbr.at[w], on_z(d))
    for w, (s, d) in enumerate(((1, 1), (0, -1))):
        rbs[2 + w] = yb[s, :, cls(d)].astype(bf16)
        rb[1, w] = send(rbs.at[2 + w], rbr.at[2 + w], on_z(d))

    for s in range(2):
        outputs(ya, s, CA, A0 + s * CA)
    ra = {}

    def reduce_y(k, way, s):
        sign = 1 if way == 0 else -1
        slot = (way * 2 + s) * 4
        value = ya[s, row(sign * (ring_steps(way, s) - k))]
        if k > 0:
            ra[way, s].wait_recv()
            value = value + rar[slot + k - 1].astype(f32)
        ras[slot + k] = value.astype(bf16)
        ra[way, s] = send(ras.at[slot + k], rar.at[slot + k], on_y(sign))

    def ra_step(k):
        for s in range(2):
            for way in range(2):
                if k < ring_steps(way, s):
                    reduce_y(k, way, s)

    ra_step(0)

    for copy in xs:
        copy.wait_recv()
    ag_sib.wait_recv()

    def spread(v):
        v = v.astype(f32).reshape(32, 8, 2 * HID)
        none = jnp.zeros((32, 8, HID), f32)
        first = jnp.concatenate([v[:, :, HID:], none], axis=2)
        second = jnp.concatenate([none, v[:, :, 0:HID]], axis=2)
        both = jnp.concatenate([first, second], axis=1)
        return both.reshape(512, 2 * HID).astype(bf16)

    mt[:, 0:512] = spread(ag[:, 0]).T
    mt[:, 512:1024] = spread(ags[...]).T

    def weight_grads(src, src_sib, s, width, first):
        for n in range(width // 256):
            lanes = slice(n * 256, (n + 1) * 256)
            lhs = src[s, :, :, :, lanes].reshape(512, 256)
            rhs = src_sib[s, :, :, :, lanes].reshape(512, 256)
            g = jnp.dot(mt[:, 0:512], lhs, preferred_element_type=f32)
            g = g + jnp.dot(mt[:, 512:1024], rhs, preferred_element_type=f32)
            cols = slice(first + n * 256, first + (n + 1) * 256)
            g1v[cols, :] = g[0:HID].T
            g2v[:, cols] = g[HID:]

    for w, (s, d) in enumerate(((0, 1), (1, -1))):
        rb[0, w].wait_recv()
        value = yb[s, :, cls(d)] + rbr[w].astype(f32)
        rbs[4 + w] = value.astype(bf16)
        rb[2, w] = send(rbs.at[4 + w], rbr.at[4 + w], on_z(d))
    ra_step(1)
    weight_grads(xa, xsa, 0, CA, A0)
    weight_grads(xa, xsa, 1, CA, A0 + CA)
    ra_step(2)
    weight_grads(xbb, xsb, 0, CB, A1)
    for w in range(2):
        rb[1, w].wait_recv()
        rb[2, w].wait_recv()
    for s in range(2):
        near = rbr[4 if s == 0 else 5].astype(f32)
        other = rbr[3 if s == 0 else 2].astype(f32)
        value = yb[s, :, zl] + near + other
        yb[s, :, zl] = value
        rys[:, s] = value.astype(bf16)
    by = []
    for d in (4, 3, 5, 2, 6, 1, 7):
        by.append(send(rys.at[row(d)], ry.at[d - 1], on_y(d)))
    ra_step(3)
    weight_grads(xbb, xsb, 1, CB, A1 + CB)
    out_g1 = pltpu.make_async_copy(g1v, g1_ref, local_sem.at[2])
    out_g2 = pltpu.make_async_copy(g2v, g2_ref, local_sem.at[3])
    out_g1.start()
    out_g2.start()

    for s in range(2):
        value = ya[s, y]
        for way in range(2):
            ra[way, s].wait_recv()
            value = value + rar[(way * 2 + s) * 4 + ring_steps(way, s) - 1].astype(f32)
        ya[s, y] = value
        rzs[s] = value.astype(bf16)
    az = []
    for w, (s, d) in enumerate(((0, 2), (1, -2))):
        az.append(send(rzs.at[s, cls(2)], rz2.at[w], on_z(d)))
    for w, d in enumerate((1, -1)):
        az.append(send(rzs.at[:, cls(d)], rz.at[w], on_z(d)))

    for copy in by:
        copy.wait_recv()
    value = yb[:, y, zl]
    for j in range(NY - 1):
        value = value + ry[j].astype(f32)
    vhb[f] = value.astype(bf16)
    last_b = [send(vhb.at[f], vhb.at[f], on_z(d)) for d in (4, -4)]
    for copy in az:
        copy.wait_recv()
    value = ya[:, y, zl] + rz[0].astype(f32) + rz[1].astype(f32)
    value = value + rz2[...].astype(f32)
    vha[f] = value.astype(bf16)
    last_a = [send(vha.at[f], vha.at[f], on_z(d)) for d in (4, -4)]

    def finish(copies, parts, width, first):
        for copy in copies:
            copy.wait_recv()
        value = parts[0].astype(f32) + parts[1].astype(f32) + parts[2].astype(f32)
        for s in range(2):
            cols = slice(first + s * width, first + (s + 1) * width)
            out_ref[:, cols] = value[s, 0:ROWS].astype(bf16)
            gtok_ref[:, cols] = value[s, 8 : 8 + ROWS].astype(bf16)

    finish(last_b, vhb, CB, A1)
    finish(last_a, vha, CA, A0)

    out_g1.wait()
    out_g2.wait()
    for copy in sent:
        copy.wait_send()


def per_device(tokens, cotangent, image_lengths, fc1_weight, fc2_weight):
    vmem = pl.BlockSpec(memory_space=pltpu.VMEM)
    smem = pl.BlockSpec(memory_space=pltpu.SMEM)
    hbm = pl.BlockSpec(memory_space=pl.ANY)

    def buf(*shape, dtype=bf16):
        return pltpu.VMEM(shape, dtype)

    return pl.pallas_call(
        kernel,
        out_shape=(
            jax.ShapeDtypeStruct((ROWS, FEAT), bf16),
            jax.ShapeDtypeStruct((ROWS, FEAT), bf16),
            jax.ShapeDtypeStruct((FEAT, HID), f32),
            jax.ShapeDtypeStruct((HID, FEAT), f32),
        ),
        in_specs=[vmem, vmem, smem, hbm, hbm],
        out_specs=(vmem, vmem, hbm, hbm),
        scratch_shapes=[
            buf(BLOCK, FEAT, dtype=f32),
            buf(2, NY, NL, BLOCK, CA),
            buf(2, NY, NL, BLOCK, CB),
            buf(2, NY, NL, BLOCK, CA),
            buf(2, NY, NL, BLOCK, CB),
            buf(FEAT, 4 * HID),
            buf(2, 2 * HID, FEAT),
            buf(3, 2, 32, 4 * HID),
            buf(3, 2, 32, 4 * HID),
            buf(2, 32, 4 * HID, dtype=f32),
            buf(NY, 2, 32, 2 * HID),
            buf(NY, 32, 2 * HID),
            buf(2, NY, NL, BLOCK, CA, dtype=f32),
            buf(2, NY, NL, BLOCK, CB, dtype=f32),
            buf(16, NL, BLOCK, CA),
            buf(16, NL, BLOCK, CA),
            buf(2, NL, BLOCK, CA),
            buf(2, 2, BLOCK, CA),
            buf(2, BLOCK, CA),
            buf(6, NY, BLOCK, CB),
            buf(6, NY, BLOCK, CB),
            buf(NY, 2, BLOCK, CB),
            buf(NY - 1, 2, BLOCK, CB),
            buf(NH, 2, BLOCK, CA),
            buf(NH, 2, BLOCK, CB),
            buf(2 * HID, 1024),
            buf(FEAT, HID, dtype=f32),
            buf(HID, FEAT, dtype=f32),
            pltpu.SemaphoreType.DMA((N_SEMS,)),
            pltpu.SemaphoreType.DMA((N_SEMS,)),
            pltpu.SemaphoreType.DMA((4,)),
        ],
        compiler_params=pltpu.CompilerParams(
            collective_id=0, has_side_effects=True, vmem_limit_bytes=48 * 1024 * 1024
        ),
    )(tokens, cotangent, image_lengths, fc1_weight, fc2_weight)


def solution(mesh):
    return jax.shard_map(
        per_device,
        mesh=mesh,
        in_specs=(
            P("tok", "fin"),
            P("tok", "fin"),
            P(),
            P("fin", ("tok", "fout")),
            P(("tok", "fout"), "fin"),
        ),
        out_specs=(
            P("tok", "fin"),
            P("tok", "fin"),
            P("fin", ("tok", "fout")),
            P(("tok", "fout"), "fin"),
        ),
        check_vma=False,
    )
```

```python
import jax
import jax.numpy as jnp
from jax import lax
from jax.experimental import pallas as pl
from jax.experimental.pallas import tpu as pltpu
from jax.sharding import PartitionSpec as P

inv_root_two = 0.7071067811865476
inv_root_two_pi = 0.3989422804014327

NX, NY, NL, NH = 4, 8, 4, 3
NZ = NL * NH
ROWS = 6
BLOCK = 16
FEAT = 1536
HID = 128
LONGEST = 48
TAIL = FEAT // 4
FOLD = FEAT - TAIL
WA = 512
WB = FOLD - WA
FAR = (4, 3, 5, 2, 6, 1, 7, 0)
N_SEMS = 80

bf16, f32 = jnp.bfloat16, jnp.float32


def place(d):
    return FAR.index(d % NY)


def sublane(v):
    return lax.broadcasted_iota(jnp.int32, v.shape, 1)


def fold(v):
    w = v.shape[2] // 4
    tail = v[:, :, 3 * w :]
    row = sublane(tail)
    segments = []
    for i in range(3):
        low = jnp.broadcast_to(tail[:, i : i + 1], tail.shape)
        high = jnp.broadcast_to(tail[:, 3 + i : 4 + i], tail.shape)
        main = v[:, :, i * w : (i + 1) * w]
        segments.append(jnp.where(row == 6, low, jnp.where(row == 7, high, main)))
    return jnp.concatenate(segments, axis=2)


def unfold(v):
    w = v.shape[2] // 3
    segments = [v[:, :, i * w : (i + 1) * w] for i in range(3)]
    row = sublane(segments[0])
    tail = jnp.zeros_like(segments[0])
    for i in range(6):
        source = segments[i % 3][:, 6 + i // 3 : 7 + i // 3]
        tail = jnp.where(row == i, jnp.broadcast_to(source, tail.shape), tail)
    real = [jnp.where(row < 6, segment, 0.0) for segment in segments]
    return jnp.concatenate(real + [tail], axis=2)


def kernel(
    tok_hbm, cot_hbm, len_hbm, w1_ref, w2_ref,
    out_ref, gtok_ref, g1_ref, g2_ref,
    tok_ref, cot_ref, len_ref, xb, pm,
    xa, xbk, xt, xsa, xsb, xst, wc, wt,
    rf, rs, rr, ag, ags,
    ysa, ysb, ray, rza, saz, rbz, sby, rby, vha, vhb,
    mt, g1v, g2v,
    send_sem, recv_sem, local_sem,
):
    t = lax.axis_index("tok")
    x = lax.axis_index("fin")
    f = lax.axis_index("fout")
    c = lax.rem(t, 2)
    y = lax.rem(lax.div(t, 2), NY)
    zl = lax.div(t, 2 * NY)
    z = f * NL + zl

    def on_y(d):
        return {"tok": (zl * NY + lax.rem(y + d + NY, NY)) * 2 + c}

    def on_z(d):
        far = lax.rem(z + d + NZ, NZ)
        return {
            "tok": (lax.rem(far, NL) * NY + y) * 2 + c,
            "fout": lax.div(far, NL),
        }

    def on_x(d):
        return {"fin": lax.rem(x + d, NX)}

    sibling = {"tok": t + 1 - 2 * c}

    sent = []

    def send(src, dst, device):
        i = len(sent)
        copy = pltpu.make_async_remote_copy(
            src_ref=src, dst_ref=dst,
            send_sem=send_sem.at[i], recv_sem=recv_sem.at[i],
            device_id=device, device_id_type=pl.DeviceIdType.MESH,
        )
        copy.start()
        sent.append(copy)
        return copy

    def arrived(copies):
        for copy in copies:
            copy.wait_recv()

    small = [
        pltpu.make_async_copy(src, dst, local_sem.at[4 + i])
        for i, (src, dst) in enumerate(
            ((len_hbm, len_ref), (cot_hbm, cot_ref), (tok_hbm, tok_ref))
        )
    ]
    for copy in small:
        copy.start()
    own_w1 = pltpu.make_async_copy(w1_ref, wc.at[:, 0:HID], local_sem.at[0])
    own_w2 = pltpu.make_async_copy(w2_ref, wt.at[0, 0:HID], local_sem.at[1])
    own_w1.start()
    own_w2.start()

    barrier = pltpu.get_barrier_semaphore()
    partners = (
        [sibling]
        + [on_x(d) for d in (1, 2, 3)]
        + [on_y(d) for d in (1, 2, 3, 4, 5, 6, 7)]
        + [on_z(d) for d in (1, -1, 2, -2, 4, -4)]
    )
    for device in partners:
        pl.semaphore_signal(
            barrier, inc=1, device_id=device, device_id_type=pl.DeviceIdType.MESH
        )

    for copy in small:
        copy.wait()
    position = t * ROWS + lax.broadcasted_iota(jnp.int32, (8, 128), 0)
    span = jnp.zeros((8, 128), jnp.int32)
    start = jnp.int32(0)
    for i in range(16):
        length = len_ref[i]
        end = start + length
        span = jnp.where((position >= start) & (position < end), length, span)
        start = end
    ratio = f32(LONGEST) / jnp.maximum(span, 1).astype(f32)
    scale = jnp.where(span > 0, jnp.sqrt(ratio), f32(0.0))
    scale = jnp.concatenate([scale] * (FEAT // 128), axis=1)[0:ROWS]
    xb[...] = jnp.zeros_like(xb)
    xb[0:ROWS] = tok_ref[...].astype(f32)
    xb[8 : 8 + ROWS] = cot_ref[...].astype(f32) * scale
    block = fold(xb[...].reshape(2, 8, FEAT)).reshape(BLOCK, FOLD).astype(bf16)
    home = place(0)
    xa[home, 0] = block[:, 0:WA]
    xbk[home, 0] = block[:, WA:]

    pl.semaphore_wait(barrier, len(partners))

    ga_z = [send(xa.at[home, 0], xa.at[home, -d % NL], on_z(d)) for d in (1, -1)]
    for d, cols in ((2, slice(0, WA // 2)), (-2, slice(WA // 2, WA))):
        ga_z.append(send(xa.at[home, 0, :, cols], xa.at[home, 2, :, cols], on_z(d)))
    gb_y = [
        send(xbk.at[home, 0], xbk.at[place(-d), 0], on_y(d)) for d in FAR[:-1]
    ]
    sib_w1 = send(w1_ref, wc.at[:, HID : 2 * HID], sibling)
    sib_w2 = send(w2_ref, wt.at[0, HID : 2 * HID], sibling)

    r = lax.broadcasted_iota(jnp.int32, (128, 384), 0)
    q = lax.broadcasted_iota(jnp.int32, (128, 384), 1)
    i = lax.rem(r, 8)
    late = jnp.where(i >= 3, 1, 0)
    spot = (i - 3 * late) * 128 + (r - i) + 6 + late
    pm[...] = jnp.where((i < 6) & (q == spot), f32(1.0), f32(0.0)).astype(bf16)
    own_w1.wait()
    own_w2.wait()
    wc[:, 2 * HID : 3 * HID] = wt[0, 0:HID].T
    wt[1, 0:HID] = wc[:, 0:HID].T

    arrived(ga_z)
    ga_y = [send(xa.at[home], xa.at[place(-d)], on_y(d)) for d in FAR[:-1]]
    arrived(gb_y)
    gb_z = [send(xbk.at[:, 0], xbk.at[:, -d % NL], on_z(d)) for d in (1, -1)]
    for d, js in ((2, slice(0, 4)), (-2, slice(4, 8))):
        gb_z.append(send(xbk.at[js, 0], xbk.at[js, 2], on_z(d)))
    arrived([sib_w1, sib_w2])
    wc[:, 3 * HID : 4 * HID] = wt[0, HID : 2 * HID].T
    wt[1, HID : 2 * HID] = wc[:, HID : 2 * HID].T
    arrived(ga_y)
    arrived(gb_z)

    def tails(dst, part_a, part_b, g):
        js = slice(2 * g, 2 * g + 2)
        whole = jnp.concatenate(
            [part_a[js].reshape(128, WA), part_b[js].reshape(128, WB)], axis=1
        )
        stacked = jnp.concatenate(
            [whole[:, i * TAIL : (i + 1) * TAIL] for i in range(3)], axis=0
        )
        value = jnp.dot(pm[...], stacked, preferred_element_type=f32)
        dst[js] = value.astype(bf16).reshape(2, NL, BLOCK, TAIL)

    def partial(h):
        tails(xt, xa, xbk, 2 * h)
        tails(xt, xa, xbk, 2 * h + 1)
        js = slice(4 * h, 4 * h + 4)
        lhs = jnp.concatenate(
            [
                xa[js].reshape(256, WA),
                xbk[js].reshape(256, WB),
                xt[js].reshape(256, TAIL),
            ],
            axis=1,
        )
        pre = jnp.dot(lhs, wc[:, 0 : 2 * HID], preferred_element_type=f32)
        back = jnp.dot(lhs, wc[:, 2 * HID : 4 * HID], preferred_element_type=f32)
        pre = pre.reshape(16, 2, 8, 2 * HID)[:, 0]
        back = back.reshape(16, 2, 8, 2 * HID)[:, 1]
        value = fold(jnp.concatenate([pre, back], axis=2)).reshape(4, 32, 3 * HID)
        rf[js] = value
        rs[js] = value.astype(bf16)

    x_in = {}
    for h in range(2):
        partial(h)
        x_in[h] = []
        for d in (2, 1, 3):
            j = 4 * h + lax.rem(x + d, NX)
            x_in[h].append(send(rs.at[j], rr.at[h, d - 1], on_x(d)))
    xs = [send(xa, xsa, sibling), send(xbk, xsb, sibling)]
    x_out = {}
    for h in range(2):
        arrived(x_in[h])
        mine = 4 * h + x
        total = rf[mine]
        for d in range(3):
            total = total + rr[h, d].astype(f32)
        total = unfold(total.reshape(4, 8, 3 * HID))
        pre, back = total[:, :, 0 : 2 * HID], total[:, :, 2 * HID : 4 * HID]
        cdf = 0.5 * (1.0 + lax.erf(pre * inv_root_two))
        density = jnp.exp(-0.5 * pre * pre) * inv_root_two_pi
        act = pre * cdf
        gp = back * (cdf + pre * density)
        value = jnp.concatenate(
            [act[:, :, 0:HID], gp[:, :, 0:HID], act[:, :, HID:], gp[:, :, HID:]],
            axis=2,
        )
        ag[mine] = fold(value).reshape(32, 3 * HID).astype(bf16)
        x_out[h] = [send(ag.at[mine], ag.at[mine], on_x(d)) for d in (2, 1, 3)]

    def outputs(h):
        js = slice(4 * h, 4 * h + 4)
        u = unfold(ag[js].astype(f32).reshape(16, 8, 3 * HID)).reshape(128, 4 * HID)
        u = u.astype(bf16)
        act2 = jnp.concatenate([u[:, 0:HID], u[:, 2 * HID : 3 * HID]], axis=1)
        gp2 = jnp.concatenate([u[:, HID : 2 * HID], u[:, 3 * HID :]], axis=1)
        fwd = jnp.dot(act2, wt[0], preferred_element_type=f32)
        bwd = jnp.dot(gp2, wt[1], preferred_element_type=f32)
        fwd = fold(fwd.reshape(16, 8, FEAT))
        bwd = fold(bwd.reshape(16, 8, FEAT))
        value = jnp.concatenate([fwd, bwd], axis=1).astype(bf16)
        ysa[js] = value[:, :, 0:WA].reshape(4, NL, BLOCK, WA)
        ysb[js] = value[:, :, WA:].reshape(4, NL, BLOCK, WB)

    ra_y, rb_z = [], []
    for h in range(2):
        arrived(x_out[h])
        outputs(h)
        js = slice(4 * h, 4 * h + 4)
        d = (2, -2)[h]
        rb_z.append(send(ysb.at[js, 2], rbz.at[2, js], on_z(d)))
        for w, d in enumerate((1, -1)):
            rb_z.append(send(ysb.at[js, d % NL], rbz.at[w, js], on_z(d)))
        for j in range(4 * h, min(4 * h + 4, NY - 1)):
            ra_y.append(send(ysa.at[j], ray.at[j], on_y(FAR[j])))

    ag_sib = send(ag, ags, sibling)

    def spread(v, lanes):
        v = unfold(v.astype(f32).reshape(32, 8, 3 * HID))[:, :, lanes]
        none = jnp.zeros((32, 8, HID), f32)
        first = jnp.concatenate([v[:, :, HID:], none], axis=2)
        second = jnp.concatenate([none, v[:, :, 0:HID]], axis=2)
        both = jnp.concatenate([first, second], axis=1)
        return both.reshape(512, 2 * HID).astype(bf16)

    mt[:, 0:512] = spread(ag[...], slice(0, 2 * HID)).T
    arrived(xs)
    for g in range(4):
        tails(xst, xsa, xsb, g)
    arrived([ag_sib])
    mt[:, 512:1024] = spread(ags[...], slice(2 * HID, 4 * HID)).T

    def weight_grads(src, src_sib, width, first):
        for n in range(0, width, 256):
            lanes = slice(n, min(n + 256, width))
            size = lanes.stop - lanes.start
            lhs = src[:, :, :, lanes].reshape(512, size)
            rhs = src_sib[:, :, :, lanes].reshape(512, size)
            g = jnp.dot(mt[:, 0:512], lhs, preferred_element_type=f32)
            g = g + jnp.dot(mt[:, 512:1024], rhs, preferred_element_type=f32)
            cols = slice(first + n, first + n + size)
            g1v[cols, :] = g[0:HID].T
            g2v[:, cols] = g[HID:]

    weight_grads(xa, xsa, WA, 0)

    arrived(rb_z)
    value = ysb[:, 0].astype(f32)
    for w in range(3):
        value = value + rbz[w].astype(f32)
    sby[...] = value.astype(bf16)
    rb_y = [send(sby.at[j], rby.at[j], on_y(FAR[j])) for j in range(NY - 1)]
    weight_grads(xbk, xsb, WB, WA)

    arrived(ra_y)
    value = ysa[home].astype(f32)
    for j in range(NY - 1):
        value = value + ray[j].astype(f32)
    saz[...] = value.astype(bf16)
    ra_z = [send(saz.at[d % NL], rza.at[w], on_z(d)) for w, d in enumerate((1, -1))]
    for d, cols in ((2, slice(0, WA // 2)), (-2, slice(WA // 2, WA))):
        ra_z.append(send(saz.at[2, :, cols], rza.at[2, :, cols], on_z(d)))
    weight_grads(xt, xst, TAIL, FOLD)
    out_g1 = pltpu.make_async_copy(g1v, g1_ref, local_sem.at[2])
    out_g2 = pltpu.make_async_copy(g2v, g2_ref, local_sem.at[3])
    out_g1.start()
    out_g2.start()

    arrived(rb_y)
    value = sby[home].astype(f32)
    for j in range(NY - 1):
        value = value + rby[j].astype(f32)
    vhb[f] = value.astype(bf16)
    last = [send(vhb.at[f], vhb.at[f], on_z(d)) for d in (4, -4)]
    arrived(ra_z)
    value = saz[0].astype(f32)
    for w in range(3):
        value = value + rza[w].astype(f32)
    vha[f] = value.astype(bf16)
    last += [send(vha.at[f], vha.at[f], on_z(d)) for d in (4, -4)]
    arrived(last)
    value = jnp.concatenate(
        [
            v[0].astype(f32) + v[1].astype(f32) + v[2].astype(f32)
            for v in (vha, vhb)
        ],
        axis=1,
    )
    value = unfold(value.reshape(2, 8, FOLD))
    out_ref[...] = value[0, 0:ROWS].astype(bf16)
    gtok_ref[...] = value[1, 0:ROWS].astype(bf16)

    out_g1.wait()
    out_g2.wait()
    for copy in sent:
        copy.wait_send()


def per_device(tokens, cotangent, image_lengths, fc1_weight, fc2_weight):
    vmem = pl.BlockSpec(memory_space=pltpu.VMEM)
    hbm = pl.BlockSpec(memory_space=pl.ANY)

    def buf(*shape, dtype=bf16):
        return pltpu.VMEM(shape, dtype)

    return pl.pallas_call(
        kernel,
        out_shape=(
            jax.ShapeDtypeStruct((ROWS, FEAT), bf16),
            jax.ShapeDtypeStruct((ROWS, FEAT), bf16),
            jax.ShapeDtypeStruct((FEAT, HID), f32),
            jax.ShapeDtypeStruct((HID, FEAT), f32),
        ),
        in_specs=[hbm] * 5,
        out_specs=(vmem, vmem, hbm, hbm),
        scratch_shapes=[
            buf(ROWS, FEAT),
            buf(ROWS, FEAT),
            pltpu.SMEM((16,), jnp.int32),
            buf(BLOCK, FEAT, dtype=f32),
            buf(128, 384),
            buf(NY, NL, BLOCK, WA),
            buf(NY, NL, BLOCK, WB),
            buf(NY, NL, BLOCK, TAIL),
            buf(NY, NL, BLOCK, WA),
            buf(NY, NL, BLOCK, WB),
            buf(NY, NL, BLOCK, TAIL),
            buf(FEAT, 4 * HID),
            buf(2, 2 * HID, FEAT),
            buf(NY, 32, 3 * HID, dtype=f32),
            buf(NY, 32, 3 * HID),
            buf(2, 3, 32, 3 * HID),
            buf(NY, 32, 3 * HID),
            buf(NY, 32, 3 * HID),
            buf(NY, NL, BLOCK, WA),
            buf(NY, NL, BLOCK, WB),
            buf(NY - 1, NL, BLOCK, WA),
            buf(3, BLOCK, WA),
            buf(NL, BLOCK, WA),
            buf(3, NY, BLOCK, WB),
            buf(NY, BLOCK, WB),
            buf(NY - 1, BLOCK, WB),
            buf(NH, BLOCK, WA),
            buf(NH, BLOCK, WB),
            buf(2 * HID, 1024),
            buf(FEAT, HID, dtype=f32),
            buf(HID, FEAT, dtype=f32),
            pltpu.SemaphoreType.DMA((N_SEMS,)),
            pltpu.SemaphoreType.DMA((N_SEMS,)),
            pltpu.SemaphoreType.DMA((8,)),
        ],
        compiler_params=pltpu.CompilerParams(
            collective_id=0, has_side_effects=True, vmem_limit_bytes=60 * 1024 * 1024
        ),
    )(tokens, cotangent, image_lengths, fc1_weight, fc2_weight)


def solution(mesh):
    return jax.shard_map(
        per_device,
        mesh=mesh,
        in_specs=(
            P("tok", "fin"),
            P("tok", "fin"),
            P(),
            P("fin", ("tok", "fout")),
            P(("tok", "fout"), "fin"),
        ),
        out_specs=(
            P("tok", "fin"),
            P("tok", "fin"),
            P("fin", ("tok", "fout")),
            P(("tok", "fout"), "fin"),
        ),
        check_vma=False,
    )
```

```python
import jax
import jax.numpy as jnp
from jax import lax
from jax.experimental import pallas as pl
from jax.experimental.pallas import tpu as pltpu
from jax.sharding import PartitionSpec as P

inv_root_two = 0.7071067811865476
inv_root_two_pi = 0.3989422804014327

NX, NY, NL, NH = 4, 8, 4, 3
NZ = NL * NH
ROWS = 6
BLOCK = 16
FEAT = 1536
HID = 128
LONGEST = 48
TAIL = FEAT // 4
FOLD = FEAT - TAIL
WA = 512
WB = FOLD - WA
WC = WA // 2
FAR = (4, 3, 5, 2, 6, 1, 7, 0)
N_SEMS = 80

bf16, f32 = jnp.bfloat16, jnp.float32


def place(d):
    return FAR.index(d % NY)


def sublane(v):
    return lax.broadcasted_iota(jnp.int32, v.shape, 1)


def fold(v):
    w = v.shape[2] // 4
    tail = v[:, :, 3 * w :]
    row = sublane(tail)
    segments = []
    for i in range(3):
        low = jnp.broadcast_to(tail[:, i : i + 1], tail.shape)
        high = jnp.broadcast_to(tail[:, 3 + i : 4 + i], tail.shape)
        main = v[:, :, i * w : (i + 1) * w]
        segments.append(jnp.where(row == 6, low, jnp.where(row == 7, high, main)))
    return jnp.concatenate(segments, axis=2)


def unfold(v):
    w = v.shape[2] // 3
    segments = [v[:, :, i * w : (i + 1) * w] for i in range(3)]
    row = sublane(segments[0])
    tail = jnp.zeros_like(segments[0])
    for i in range(6):
        source = segments[i % 3][:, 6 + i // 3 : 7 + i // 3]
        tail = jnp.where(row == i, jnp.broadcast_to(source, tail.shape), tail)
    real = [jnp.where(row < 6, segment, 0.0) for segment in segments]
    return jnp.concatenate(real + [tail], axis=2)


def kernel(
    tok_hbm, cot_hbm, len_hbm, w1_ref, w2_ref,
    out_ref, gtok_ref, g1v, g2v,
    tok_ref, cot_ref, len_ref, xb, pm,
    xa, xbk, xt, xsa, xsb, xst, wc, wt,
    rf, rs, rr, ag, ags,
    ysa, ysb, rel, rel2, ray, rza, saz, rbz, sby, rby, vha, vhb,
    mt,
    send_sem, recv_sem, local_sem,
):
    t = lax.axis_index("tok")
    x = lax.axis_index("fin")
    f = lax.axis_index("fout")
    c = lax.rem(t, 2)
    y = lax.rem(lax.div(t, 2), NY)
    zl = lax.div(t, 2 * NY)
    z = f * NL + zl

    def on_y(d):
        return {"tok": (zl * NY + lax.rem(y + d + NY, NY)) * 2 + c}

    def on_z(d):
        far = lax.rem(z + d + NZ, NZ)
        return {
            "tok": (lax.rem(far, NL) * NY + y) * 2 + c,
            "fout": lax.div(far, NL),
        }

    def on_x(d):
        return {"fin": lax.rem(x + d, NX)}

    sibling = {"tok": t + 1 - 2 * c}

    sent = []

    def send(src, dst, device):
        i = len(sent)
        copy = pltpu.make_async_remote_copy(
            src_ref=src, dst_ref=dst,
            send_sem=send_sem.at[i], recv_sem=recv_sem.at[i],
            device_id=device, device_id_type=pl.DeviceIdType.MESH,
        )
        copy.start()
        sent.append(copy)
        return copy

    def arrived(copies):
        for copy in copies:
            copy.wait_recv()

    small = [
        pltpu.make_async_copy(src, dst, local_sem.at[4 + i])
        for i, (src, dst) in enumerate(
            ((len_hbm, len_ref), (cot_hbm, cot_ref), (tok_hbm, tok_ref))
        )
    ]
    for copy in small:
        copy.start()
    own_w1 = pltpu.make_async_copy(w1_ref, wc.at[:, 0:HID], local_sem.at[0])
    own_w2 = pltpu.make_async_copy(w2_ref, wt.at[0, 0:HID], local_sem.at[1])
    own_w1.start()
    own_w2.start()

    barrier = pltpu.get_barrier_semaphore()
    partners = (
        [sibling]
        + [on_x(d) for d in (1, 2, 3)]
        + [on_y(d) for d in (1, 2, 3, 4, 5, 6, 7)]
        + [on_z(d) for d in (1, -1, 2, -2, 4, -4)]
    )
    for device in partners:
        pl.semaphore_signal(
            barrier, inc=1, device_id=device, device_id_type=pl.DeviceIdType.MESH
        )

    for copy in small:
        copy.wait()
    position = t * ROWS + lax.broadcasted_iota(jnp.int32, (8, 128), 0)
    span = jnp.zeros((8, 128), jnp.int32)
    start = jnp.int32(0)
    for i in range(16):
        length = len_ref[i]
        end = start + length
        span = jnp.where((position >= start) & (position < end), length, span)
        start = end
    ratio = f32(LONGEST) / jnp.maximum(span, 1).astype(f32)
    scale = jnp.where(span > 0, jnp.sqrt(ratio), f32(0.0))
    scale = jnp.concatenate([scale] * (FEAT // 128), axis=1)[0:ROWS]
    xb[...] = jnp.zeros_like(xb)
    xb[0:ROWS] = tok_ref[...].astype(f32)
    xb[8 : 8 + ROWS] = cot_ref[...].astype(f32) * scale
    block = fold(xb[...].reshape(2, 8, FEAT)).reshape(BLOCK, FOLD).astype(bf16)
    home = place(0)
    xa[home, 0] = block[:, 0:WA]
    xbk[home, 0] = block[:, WA:]

    pl.semaphore_wait(barrier, len(partners))

    ga_z = [send(xa.at[home, 0], xa.at[home, -d % NL], on_z(d)) for d in (1, -1)]
    for d, cols in ((2, slice(0, WC)), (-2, slice(WC, WA))):
        ga_z.append(send(xa.at[home, 0, :, cols], xa.at[home, 2, :, cols], on_z(d)))
    gb_y = [
        send(xbk.at[home, 0], xbk.at[place(-d), 0], on_y(d)) for d in FAR[:-1]
    ]
    sib_w1 = send(w1_ref, wc.at[:, HID : 2 * HID], sibling)
    sib_w2 = send(w2_ref, wt.at[0, HID : 2 * HID], sibling)

    r = lax.broadcasted_iota(jnp.int32, (128, 384), 0)
    q = lax.broadcasted_iota(jnp.int32, (128, 384), 1)
    i = lax.rem(r, 8)
    late = jnp.where(i >= 3, 1, 0)
    spot = (i - 3 * late) * 128 + (r - i) + 6 + late
    pm[...] = jnp.where((i < 6) & (q == spot), f32(1.0), f32(0.0)).astype(bf16)
    own_w1.wait()
    own_w2.wait()
    wc[:, 2 * HID : 3 * HID] = wt[0, 0:HID].T
    wt[1, 0:HID] = wc[:, 0:HID].T

    arrived(ga_z)
    ga_y = {d: send(xa.at[home], xa.at[place(-d)], on_y(d)) for d in (2, -2, 1, -1)}
    arrived(gb_y)
    gb_z = [send(xbk.at[:, 0], xbk.at[:, -d % NL], on_z(d)) for d in (1, -1)]
    for d, js in ((2, slice(0, 4)), (-2, slice(4, 8))):
        gb_z.append(send(xbk.at[js, 0], xbk.at[js, 2], on_z(d)))
    ga_far = []
    for way, ks in ((1, slice(0, 2)), (-1, slice(2, 4))):
        arrived([ga_y[2 * way]])
        group = place(-2 * way)
        ga_far.append(
            send(xa.at[group, ks], xa.at[place(4), ks], on_y(2 * way))
        )
        ga_far.append(send(xa.at[group], xa.at[place(-3 * way)], on_y(way)))
    arrived([sib_w1, sib_w2])
    wc[:, 3 * HID : 4 * HID] = wt[0, HID : 2 * HID].T
    wt[1, HID : 2 * HID] = wc[:, HID : 2 * HID].T
    arrived([ga_y[1], ga_y[-1]] + ga_far)
    arrived(gb_z)

    def tails(dst, part_a, part_b, g):
        js = slice(2 * g, 2 * g + 2)
        whole = jnp.concatenate(
            [part_a[js].reshape(128, WA), part_b[js].reshape(128, WB)], axis=1
        )
        stacked = jnp.concatenate(
            [whole[:, i * TAIL : (i + 1) * TAIL] for i in range(3)], axis=0
        )
        value = jnp.dot(pm[...], stacked, preferred_element_type=f32)
        dst[js] = value.astype(bf16).reshape(2, NL, BLOCK, TAIL)

    def partial(h):
        tails(xt, xa, xbk, 2 * h)
        tails(xt, xa, xbk, 2 * h + 1)
        js = slice(4 * h, 4 * h + 4)
        lhs = jnp.concatenate(
            [
                xa[js].reshape(256, WA),
                xbk[js].reshape(256, WB),
                xt[js].reshape(256, TAIL),
            ],
            axis=1,
        )
        pre = jnp.dot(lhs, wc[:, 0 : 2 * HID], preferred_element_type=f32)
        back = jnp.dot(lhs, wc[:, 2 * HID : 4 * HID], preferred_element_type=f32)
        pre = pre.reshape(16, 2, 8, 2 * HID)[:, 0]
        back = back.reshape(16, 2, 8, 2 * HID)[:, 1]
        value = fold(jnp.concatenate([pre, back], axis=2)).reshape(4, 32, 3 * HID)
        rf[js] = value
        rs[js] = value.astype(bf16)

    x_in = {}
    for h in range(2):
        partial(h)
        x_in[h] = []
        for d in (2, 1, 3):
            j = 4 * h + lax.rem(x + d, NX)
            x_in[h].append(send(rs.at[j], rr.at[h, d - 1], on_x(d)))
    xs = [send(xa, xsa, sibling), send(xbk, xsb, sibling)]
    x_out = {}
    for h in range(2):
        arrived(x_in[h])
        mine = 4 * h + x
        total = rf[mine]
        for d in range(3):
            total = total + rr[h, d].astype(f32)
        total = unfold(total.reshape(4, 8, 3 * HID))
        pre, back = total[:, :, 0 : 2 * HID], total[:, :, 2 * HID : 4 * HID]
        cdf = 0.5 * (1.0 + lax.erf(pre * inv_root_two))
        density = jnp.exp(-0.5 * pre * pre) * inv_root_two_pi
        act = pre * cdf
        gp = back * (cdf + pre * density)
        value = jnp.concatenate(
            [act[:, :, 0:HID], gp[:, :, 0:HID], act[:, :, HID:], gp[:, :, HID:]],
            axis=2,
        )
        ag[mine] = fold(value).reshape(32, 3 * HID).astype(bf16)
        x_out[h] = [send(ag.at[mine], ag.at[mine], on_x(d)) for d in (2, 1, 3)]

    def outputs(h):
        js = slice(4 * h, 4 * h + 4)
        u = unfold(ag[js].astype(f32).reshape(16, 8, 3 * HID)).reshape(128, 4 * HID)
        u = u.astype(bf16)
        act2 = jnp.concatenate([u[:, 0:HID], u[:, 2 * HID : 3 * HID]], axis=1)
        gp2 = jnp.concatenate([u[:, HID : 2 * HID], u[:, 3 * HID :]], axis=1)
        fwd = jnp.dot(act2, wt[0], preferred_element_type=f32)
        bwd = jnp.dot(gp2, wt[1], preferred_element_type=f32)
        fwd = fold(fwd.reshape(16, 8, FEAT))
        bwd = fold(bwd.reshape(16, 8, FEAT))
        value = jnp.concatenate([fwd, bwd], axis=1).astype(bf16)
        ysa[js] = value[:, :, 0:WA].reshape(4, NL, BLOCK, WA)
        ysb[js] = value[:, :, WA:].reshape(4, NL, BLOCK, WB)

    ra_y, rb_z, relay = [], [], []
    for h in range(2):
        arrived(x_out[h])
        outputs(h)
        js = slice(4 * h, 4 * h + 4)
        d = (2, -2)[h]
        rb_z.append(send(ysb.at[js, 2], rbz.at[2, js], on_z(d)))
        for w, d in enumerate((1, -1)):
            rb_z.append(send(ysb.at[js, d % NL], rbz.at[w, js], on_z(d)))
        for way, ks in ((1, slice(0, 2)), (-1, slice(2, 4))):
            w = (1 - way) // 2
            if h == 0:
                relay.append(send(ysa.at[place(3 * way)], rel.at[w], on_y(way)))
                far = send(ysa.at[place(4), ks], rel.at[2 + w, ks], on_y(2 * way))
                relay.append(far)
            else:
                ra_y.append(send(ysa.at[place(way)], ray.at[w], on_y(way)))

    arrived(relay)
    for way, ks in ((1, slice(0, 2)), (-1, slice(2, 4))):
        w = (1 - way) // 2
        value = ysa[place(2 * way)].astype(f32) + rel[w].astype(f32)
        extra = rel[2 + w, ks].astype(f32)
        rel2[w] = value.astype(bf16)
        rel2[w, ks] = (value[ks] + extra).astype(bf16)
        ra_y.append(send(rel2.at[w], ray.at[2 + w], on_y(2 * way)))

    ag_sib = send(ag, ags, sibling)

    def spread(v, lanes):
        v = unfold(v.astype(f32).reshape(32, 8, 3 * HID))[:, :, lanes]
        none = jnp.zeros((32, 8, HID), f32)
        first = jnp.concatenate([v[:, :, HID:], none], axis=2)
        second = jnp.concatenate([none, v[:, :, 0:HID]], axis=2)
        both = jnp.concatenate([first, second], axis=1)
        return both.reshape(512, 2 * HID).astype(bf16)

    mt[:, 0:512] = spread(ag[...], slice(0, 2 * HID)).T
    arrived(xs)
    for g in range(4):
        tails(xst, xsa, xsb, g)
    arrived([ag_sib])
    mt[:, 512:1024] = spread(ags[...], slice(2 * HID, 4 * HID)).T

    def weight_grads(src, src_sib, width, first):
        for n in range(0, width, 256):
            lanes = slice(n, min(n + 256, width))
            size = lanes.stop - lanes.start
            lhs = src[:, :, :, lanes].reshape(512, size)
            rhs = src_sib[:, :, :, lanes].reshape(512, size)
            g = jnp.dot(mt[:, 0:512], lhs, preferred_element_type=f32)
            g = g + jnp.dot(mt[:, 512:1024], rhs, preferred_element_type=f32)
            cols = slice(first + n, first + n + size)
            g1v[cols, :] = g[0:HID].T
            g2v[:, cols] = g[HID:]

    weight_grads(xa, xsa, WA, 0)

    arrived(rb_z)
    value = ysb[:, 0].astype(f32)
    for w in range(3):
        value = value + rbz[w].astype(f32)
    sby[...] = value.astype(bf16)
    rb_y = [send(sby.at[j], rby.at[j], on_y(FAR[j])) for j in range(NY - 1)]
    weight_grads(xbk, xsb, WB, WA)

    arrived(ra_y)
    value = ysa[home].astype(f32)
    for j in range(4):
        value = value + ray[j].astype(f32)
    saz[...] = value.astype(bf16)
    ra_z = [send(saz.at[d % NL], rza.at[w], on_z(d)) for w, d in enumerate((1, -1))]
    for d, cols in ((2, slice(0, WC)), (-2, slice(WC, WA))):
        ra_z.append(send(saz.at[2, :, cols], rza.at[2, :, cols], on_z(d)))
    weight_grads(xt, xst, TAIL, FOLD)

    arrived(rb_y)
    value = sby[home].astype(f32)
    for j in range(NY - 1):
        value = value + rby[j].astype(f32)
    vhb[f] = value.astype(bf16)
    last = [send(vhb.at[f], vhb.at[f], on_z(d)) for d in (4, -4)]
    arrived(ra_z)
    value = saz[0].astype(f32)
    for w in range(3):
        value = value + rza[w].astype(f32)
    vha[f] = value.astype(bf16)
    last += [send(vha.at[f], vha.at[f], on_z(d)) for d in (4, -4)]
    arrived(last)
    value = jnp.concatenate(
        [
            v[0].astype(f32) + v[1].astype(f32) + v[2].astype(f32)
            for v in (vha, vhb)
        ],
        axis=1,
    )
    value = unfold(value.reshape(2, 8, FOLD))
    out_ref[...] = value[0, 0:ROWS].astype(bf16)
    gtok_ref[...] = value[1, 0:ROWS].astype(bf16)

    for copy in sent:
        copy.wait_send()


def write_out(*refs):
    sem = refs[8]
    copies = [pltpu.make_async_copy(refs[i], refs[4 + i], sem.at[i]) for i in range(4)]
    for copy in copies:
        copy.start()
    for copy in copies:
        copy.wait()


def per_device(tokens, cotangent, image_lengths, fc1_weight, fc2_weight):
    vmem = pl.BlockSpec(memory_space=pltpu.VMEM)
    hbm = pl.BlockSpec(memory_space=pl.ANY)

    def buf(*shape, dtype=bf16):
        return pltpu.VMEM(shape, dtype)

    shapes = (
        ((ROWS, FEAT), bf16),
        ((ROWS, FEAT), bf16),
        ((FEAT, HID), f32),
        ((HID, FEAT), f32),
    )
    arguments = [
        pltpu.with_memory_space_constraint(a, pltpu.HBM)
        for a in (tokens, cotangent, image_lengths, fc1_weight, fc2_weight)
    ]
    results = pl.pallas_call(
        kernel,
        out_shape=tuple(pltpu.VMEM(*shape) for shape in shapes),
        in_specs=[hbm] * 5,
        out_specs=(vmem,) * 4,
        scratch_shapes=[
            buf(ROWS, FEAT),
            buf(ROWS, FEAT),
            pltpu.SMEM((16,), jnp.int32),
            buf(BLOCK, FEAT, dtype=f32),
            buf(128, 384),
            buf(NY, NL, BLOCK, WA),
            buf(NY, NL, BLOCK, WB),
            buf(NY, NL, BLOCK, TAIL),
            buf(NY, NL, BLOCK, WA),
            buf(NY, NL, BLOCK, WB),
            buf(NY, NL, BLOCK, TAIL),
            buf(FEAT, 4 * HID),
            buf(2, 2 * HID, FEAT),
            buf(NY, 32, 3 * HID, dtype=f32),
            buf(NY, 32, 3 * HID),
            buf(2, 3, 32, 3 * HID),
            buf(NY, 32, 3 * HID),
            buf(NY, 32, 3 * HID),
            buf(NY, NL, BLOCK, WA),
            buf(NY, NL, BLOCK, WB),
            buf(4, NL, BLOCK, WA),
            buf(2, NL, BLOCK, WA),
            buf(4, NL, BLOCK, WA),
            buf(3, BLOCK, WA),
            buf(NL, BLOCK, WA),
            buf(3, NY, BLOCK, WB),
            buf(NY, BLOCK, WB),
            buf(NY - 1, BLOCK, WB),
            buf(NH, BLOCK, WA),
            buf(NH, BLOCK, WB),
            buf(2 * HID, 1024),
            pltpu.SemaphoreType.DMA((N_SEMS,)),
            pltpu.SemaphoreType.DMA((N_SEMS,)),
            pltpu.SemaphoreType.DMA((8,)),
        ],
        compiler_params=pltpu.CompilerParams(
            collective_id=0, has_side_effects=True, vmem_limit_bytes=44 * 1024 * 1024
        ),
    )(*arguments)
    return pl.pallas_call(
        write_out,
        out_shape=tuple(jax.ShapeDtypeStruct(*shape) for shape in shapes),
        in_specs=[vmem] * 4,
        out_specs=(hbm,) * 4,
        scratch_shapes=[pltpu.SemaphoreType.DMA((4,))],
        compiler_params=pltpu.CompilerParams(vmem_limit_bytes=4 * 1024 * 1024),
    )(*results)


def solution(mesh):
    return jax.shard_map(
        per_device,
        mesh=mesh,
        in_specs=(
            P("tok", "fin"),
            P("tok", "fin"),
            P(),
            P("fin", ("tok", "fout")),
            P(("tok", "fout"), "fin"),
        ),
        out_specs=(
            P("tok", "fin"),
            P("tok", "fin"),
            P("fin", ("tok", "fout")),
            P(("tok", "fout"), "fin"),
        ),
        check_vma=False,
    )
```

```python
import jax
import jax.numpy as jnp
from jax import lax
from jax.experimental import pallas as pl
from jax.experimental.pallas import tpu as pltpu
from jax.sharding import PartitionSpec as P

inv_root_two = 0.7071067811865476
inv_root_two_pi = 0.3989422804014327

NX, NY, NL, NH = 4, 8, 4, 3
NZ = NL * NH
ROWS = 6
BLOCK = 16
FEAT = 1536
HID = 128
LONGEST = 48
TAIL = FEAT // 4
FOLD = FEAT - TAIL
WA = 512
WB = FOLD - WA
WC = 256
RA = 384
RB = FOLD - RA
RC = 128
FAR = (4, 3, 5, 2, 6, 1, 7, 0)
N_SEMS = 80

bf16, f32 = jnp.bfloat16, jnp.float32


def place(d):
    return FAR.index(d % NY)


def sublane(v):
    return lax.broadcasted_iota(jnp.int32, v.shape, 1)


def fold(v):
    w = v.shape[2] // 4
    tail = v[:, :, 3 * w :]
    row = sublane(tail)
    segments = []
    for i in range(3):
        low = jnp.broadcast_to(tail[:, i : i + 1], tail.shape)
        high = jnp.broadcast_to(tail[:, 3 + i : 4 + i], tail.shape)
        main = v[:, :, i * w : (i + 1) * w]
        segments.append(jnp.where(row == 6, low, jnp.where(row == 7, high, main)))
    return jnp.concatenate(segments, axis=2)


def unfold(v):
    w = v.shape[2] // 3
    segments = [v[:, :, i * w : (i + 1) * w] for i in range(3)]
    row = sublane(segments[0])
    tail = jnp.zeros_like(segments[0])
    for i in range(6):
        source = segments[i % 3][:, 6 + i // 3 : 7 + i // 3]
        tail = jnp.where(row == i, jnp.broadcast_to(source, tail.shape), tail)
    real = [jnp.where(row < 6, segment, 0.0) for segment in segments]
    return jnp.concatenate(real + [tail], axis=2)


def kernel(
    tok_hbm, cot_hbm, len_hbm, w1_ref, w2_ref,
    out_ref, gtok_ref, g1v, g2v,
    tok_ref, cot_ref, len_ref, xb, pm,
    xa, xbk, xt, xsa, xsb, xst, wc, wt,
    rf, rs, rr, ag, ags,
    ysa, ysb, ray, rza, saz, rbz, sby, rby, vha, vhb,
    mt,
    send_sem, recv_sem, local_sem,
):
    t = lax.axis_index("tok")
    x = lax.axis_index("fin")
    f = lax.axis_index("fout")
    c = lax.rem(t, 2)
    y = lax.rem(lax.div(t, 2), NY)
    zl = lax.div(t, 2 * NY)
    z = f * NL + zl

    def on_y(d):
        return {"tok": (zl * NY + lax.rem(y + d + NY, NY)) * 2 + c}

    def on_z(d):
        far = lax.rem(z + d + NZ, NZ)
        return {
            "tok": (lax.rem(far, NL) * NY + y) * 2 + c,
            "fout": lax.div(far, NL),
        }

    def on_x(d):
        return {"fin": lax.rem(x + d, NX)}

    sibling = {"tok": t + 1 - 2 * c}

    sent = []

    def send(src, dst, device):
        i = len(sent)
        copy = pltpu.make_async_remote_copy(
            src_ref=src, dst_ref=dst,
            send_sem=send_sem.at[i], recv_sem=recv_sem.at[i],
            device_id=device, device_id_type=pl.DeviceIdType.MESH,
        )
        copy.start()
        sent.append(copy)
        return copy

    def arrived(copies):
        for copy in copies:
            copy.wait_recv()

    small = [
        pltpu.make_async_copy(src, dst, local_sem.at[4 + i])
        for i, (src, dst) in enumerate(
            ((len_hbm, len_ref), (cot_hbm, cot_ref), (tok_hbm, tok_ref))
        )
    ]
    for copy in small:
        copy.start()
    own_w1 = pltpu.make_async_copy(w1_ref, wc.at[:, 0:HID], local_sem.at[0])
    own_w2 = pltpu.make_async_copy(w2_ref, wt.at[0, 0:HID], local_sem.at[1])
    own_w1.start()
    own_w2.start()

    barrier = pltpu.get_barrier_semaphore()
    partners = (
        [sibling]
        + [on_x(d) for d in (1, 2, 3)]
        + [on_y(d) for d in (1, 2, 3, 4, 5, 6, 7)]
        + [on_z(d) for d in (1, -1, 2, -2, 4, -4)]
    )
    for device in partners:
        pl.semaphore_signal(
            barrier, inc=1, device_id=device, device_id_type=pl.DeviceIdType.MESH
        )

    for copy in small:
        copy.wait()
    position = t * ROWS + lax.broadcasted_iota(jnp.int32, (8, 128), 0)
    span = jnp.zeros((8, 128), jnp.int32)
    start = jnp.int32(0)
    for i in range(16):
        length = len_ref[i]
        end = start + length
        span = jnp.where((position >= start) & (position < end), length, span)
        start = end
    ratio = f32(LONGEST) / jnp.maximum(span, 1).astype(f32)
    scale = jnp.where(span > 0, jnp.sqrt(ratio), f32(0.0))
    scale = jnp.concatenate([scale] * (FEAT // 128), axis=1)[0:ROWS]
    xb[...] = jnp.zeros_like(xb)
    xb[0:ROWS] = tok_ref[...].astype(f32)
    xb[8 : 8 + ROWS] = cot_ref[...].astype(f32) * scale
    block = fold(xb[...].reshape(2, 8, FEAT)).reshape(BLOCK, FOLD).astype(bf16)
    home = place(0)
    xa[home, 0] = block[:, 0:WA]
    xbk[home, 0] = block[:, WA:]

    pl.semaphore_wait(barrier, len(partners))

    ga_z = [send(xa.at[home, 0], xa.at[home, -d % NL], on_z(d)) for d in (1, -1)]
    for d, cols in ((2, slice(0, WC)), (-2, slice(WC, WA))):
        ga_z.append(send(xa.at[home, 0, :, cols], xa.at[home, 2, :, cols], on_z(d)))
    gb_y = {
        place(-d): send(xbk.at[home, 0], xbk.at[place(-d), 0], on_y(d))
        for d in (2, 1, -1, -2, 4, 3, -3)
    }

    r = lax.broadcasted_iota(jnp.int32, (128, 384), 0)
    q = lax.broadcasted_iota(jnp.int32, (128, 384), 1)
    i = lax.rem(r, 8)
    late = jnp.where(i >= 3, 1, 0)
    spot = (i - 3 * late) * 128 + (r - i) + 6 + late
    pm[...] = jnp.where((i < 6) & (q == spot), f32(1.0), f32(0.0)).astype(bf16)
    own_w1.wait()
    own_w2.wait()
    wc[:, 2 * HID : 3 * HID] = wt[0, 0:HID].T
    wt[1, 0:HID] = wc[:, 0:HID].T

    arrived(ga_z)
    ga_y = {d: send(xa.at[home], xa.at[place(-d)], on_y(d)) for d in (2, -2, 1, -1)}
    sib_w1 = send(w1_ref, wc.at[:, HID : 2 * HID], sibling)
    sib_w2 = send(w2_ref, wt.at[0, HID : 2 * HID], sibling)
    gb_z = []
    for js, d in ((slice(4, 8), -2), (slice(0, 4), 2)):
        arrived([gb_y[j] for j in range(js.start, js.stop) if j != home])
        for to in (d, 1, -1):
            gb_z.append(send(xbk.at[js, 0], xbk.at[js, -to % NL], on_z(to)))
    ga_far = []
    for way, ks in ((1, slice(0, 2)), (-1, slice(2, 4))):
        arrived([ga_y[2 * way]])
        group = place(-2 * way)
        ga_far.append(
            send(xa.at[group, ks], xa.at[place(4), ks], on_y(2 * way))
        )
        ga_far.append(send(xa.at[group], xa.at[place(-3 * way)], on_y(way)))
    arrived([sib_w1, sib_w2])
    wc[:, 3 * HID : 4 * HID] = wt[0, HID : 2 * HID].T
    wt[1, HID : 2 * HID] = wc[:, HID : 2 * HID].T
    arrived([ga_y[1], ga_y[-1]] + ga_far)
    arrived(gb_z)

    def tails(dst, part_a, part_b, g):
        js = slice(2 * g, 2 * g + 2)
        whole = jnp.concatenate(
            [part_a[js].reshape(128, WA), part_b[js].reshape(128, WB)], axis=1
        )
        stacked = jnp.concatenate(
            [whole[:, i * TAIL : (i + 1) * TAIL] for i in range(3)], axis=0
        )
        value = jnp.dot(pm[...], stacked, preferred_element_type=f32)
        dst[js] = value.astype(bf16).reshape(2, NL, BLOCK, TAIL)

    def partial(h):
        tails(xt, xa, xbk, 2 * h)
        tails(xt, xa, xbk, 2 * h + 1)
        js = slice(4 * h, 4 * h + 4)
        lhs = jnp.concatenate(
            [
                xa[js].reshape(256, WA),
                xbk[js].reshape(256, WB),
                xt[js].reshape(256, TAIL),
            ],
            axis=1,
        )
        pre = jnp.dot(lhs, wc[:, 0 : 2 * HID], preferred_element_type=f32)
        back = jnp.dot(lhs, wc[:, 2 * HID : 4 * HID], preferred_element_type=f32)
        pre = pre.reshape(16, 2, 8, 2 * HID)[:, 0]
        back = back.reshape(16, 2, 8, 2 * HID)[:, 1]
        value = fold(jnp.concatenate([pre, back], axis=2)).reshape(4, 32, 3 * HID)
        rf[js] = value
        rs[js] = value.astype(bf16)

    x_in = {}
    for h in range(2):
        partial(h)
        x_in[h] = []
        for d in (2, 1, 3):
            j = 4 * h + lax.rem(x + d, NX)
            x_in[h].append(send(rs.at[j], rr.at[h, d - 1], on_x(d)))
    xs = [send(xa, xsa, sibling), send(xbk, xsb, sibling)]
    x_out = {}
    for h in range(2):
        arrived(x_in[h])
        mine = 4 * h + x
        total = rf[mine]
        for d in range(3):
            total = total + rr[h, d].astype(f32)
        total = unfold(total.reshape(4, 8, 3 * HID))
        pre, back = total[:, :, 0 : 2 * HID], total[:, :, 2 * HID : 4 * HID]
        cdf = 0.5 * (1.0 + lax.erf(pre * inv_root_two))
        density = jnp.exp(-0.5 * pre * pre) * inv_root_two_pi
        act = pre * cdf
        gp = back * (cdf + pre * density)
        value = jnp.concatenate(
            [act[:, :, 0:HID], gp[:, :, 0:HID], act[:, :, HID:], gp[:, :, HID:]],
            axis=2,
        )
        ag[mine] = fold(value).reshape(32, 3 * HID).astype(bf16)
        x_out[h] = [send(ag.at[mine], ag.at[mine], on_x(d)) for d in (2, 1, 3)]

    arrived(xs)
    for g in range(4):
        tails(xst, xsa, xsb, g)

    def outputs(h):
        js = slice(4 * h, 4 * h + 4)
        u = unfold(ag[js].astype(f32).reshape(16, 8, 3 * HID)).reshape(128, 4 * HID)
        u = u.astype(bf16)
        act2 = jnp.concatenate([u[:, 0:HID], u[:, 2 * HID : 3 * HID]], axis=1)
        gp2 = jnp.concatenate([u[:, HID : 2 * HID], u[:, 3 * HID :]], axis=1)
        fwd = jnp.dot(act2, wt[0], preferred_element_type=f32)
        bwd = jnp.dot(gp2, wt[1], preferred_element_type=f32)
        fwd = fold(fwd.reshape(16, 8, FEAT))
        bwd = fold(bwd.reshape(16, 8, FEAT))
        value = jnp.concatenate([fwd, bwd], axis=1).astype(bf16)
        ysa[js] = value[:, :, 0:RA].reshape(4, NL, BLOCK, RA)
        ysb[js] = value[:, :, RA:].reshape(4, NL, BLOCK, RB)

    ra_y, rb_z = [], ([], [])
    for h in range(2):
        arrived(x_out[h])
        outputs(h)
        js = slice(4 * h, 4 * h + 4)
        for j in range(4 * h, min(4 * h + 4, NY - 1)):
            ra_y.append(send(ysa.at[j], ray.at[j], on_y(FAR[j])))
        d = (2, -2)[h]
        rb_z[h].append(send(ysb.at[js, 2], rbz.at[2, js], on_z(d)))
        for w, d in enumerate((1, -1)):
            rb_z[h].append(send(ysb.at[js, d % NL], rbz.at[w, js], on_z(d)))

    ag_sib = send(ag, ags, sibling)

    def spread(v, lanes):
        v = unfold(v.astype(f32).reshape(32, 8, 3 * HID))[:, :, lanes]
        none = jnp.zeros((32, 8, HID), f32)
        first = jnp.concatenate([v[:, :, HID:], none], axis=2)
        second = jnp.concatenate([none, v[:, :, 0:HID]], axis=2)
        both = jnp.concatenate([first, second], axis=1)
        return both.reshape(512, 2 * HID).astype(bf16)

    def part_b_y(h):
        arrived(rb_z[h])
        js = slice(4 * h, 4 * h + 4)
        value = ysb[js, 0].astype(f32)
        for w in range(3):
            value = value + rbz[w, js].astype(f32)
        sby[js] = value.astype(bf16)
        return [
            send(sby.at[j], rby.at[j], on_y(FAR[j]))
            for j in range(4 * h, min(4 * h + 4, NY - 1))
        ]

    rb_y = part_b_y(0)
    rb_y += part_b_y(1)
    mt[:, 0:512] = spread(ag[...], slice(0, 2 * HID)).T

    def weight_grads(src, src_sib, width, first):
        for n in range(0, width, 256):
            lanes = slice(n, min(n + 256, width))
            size = lanes.stop - lanes.start
            lhs = src[:, :, :, lanes].reshape(512, size)
            rhs = src_sib[:, :, :, lanes].reshape(512, size)
            g = jnp.dot(mt[:, 0:512], lhs, preferred_element_type=f32)
            g = g + jnp.dot(mt[:, 512:1024], rhs, preferred_element_type=f32)
            cols = slice(first + n, first + n + size)
            g1v[cols, :] = g[0:HID].T
            g2v[:, cols] = g[HID:]


    arrived([ag_sib])
    mt[:, 512:1024] = spread(ags[...], slice(2 * HID, 4 * HID)).T

    arrived(ra_y)
    value = ysa[home].astype(f32)
    for j in range(NY - 1):
        value = value + ray[j].astype(f32)
    saz[...] = value.astype(bf16)
    ra_z = [send(saz.at[d % NL], rza.at[w], on_z(d)) for w, d in enumerate((1, -1))]
    for d, cols in ((2, slice(0, RC)), (-2, slice(RC, RA))):
        ra_z.append(send(saz.at[2, :, cols], rza.at[2, :, cols], on_z(d)))
    weight_grads(xt, xst, TAIL, FOLD)

    arrived(rb_y)
    value = sby[home].astype(f32)
    for j in range(NY - 1):
        value = value + rby[j].astype(f32)
    vhb[f] = value.astype(bf16)
    last = [send(vhb.at[f], vhb.at[f], on_z(d)) for d in (4, -4)]
    arrived(ra_z)
    value = saz[0].astype(f32)
    for w in range(3):
        value = value + rza[w].astype(f32)
    vha[f] = value.astype(bf16)
    last += [send(vha.at[f], vha.at[f], on_z(d)) for d in (4, -4)]
    weight_grads(xa, xsa, WA, 0)
    weight_grads(xbk, xsb, WB, WA)
    arrived(last)
    value = jnp.concatenate(
        [
            v[0].astype(f32) + v[1].astype(f32) + v[2].astype(f32)
            for v in (vha, vhb)
        ],
        axis=1,
    )
    value = unfold(value.reshape(2, 8, FOLD))
    out_ref[...] = value[0, 0:ROWS].astype(bf16)
    gtok_ref[...] = value[1, 0:ROWS].astype(bf16)

    for copy in sent:
        copy.wait_send()


def write_out(*refs):
    sem = refs[8]
    copies = [pltpu.make_async_copy(refs[i], refs[4 + i], sem.at[i]) for i in range(4)]
    for copy in copies:
        copy.start()
    for copy in copies:
        copy.wait()


def per_device(tokens, cotangent, image_lengths, fc1_weight, fc2_weight):
    vmem = pl.BlockSpec(memory_space=pltpu.VMEM)
    hbm = pl.BlockSpec(memory_space=pl.ANY)

    def buf(*shape, dtype=bf16):
        return pltpu.VMEM(shape, dtype)

    shapes = (
        ((ROWS, FEAT), bf16),
        ((ROWS, FEAT), bf16),
        ((FEAT, HID), f32),
        ((HID, FEAT), f32),
    )
    arguments = [
        pltpu.with_memory_space_constraint(a, pltpu.HBM)
        for a in (tokens, cotangent, image_lengths, fc1_weight, fc2_weight)
    ]
    results = pl.pallas_call(
        kernel,
        out_shape=tuple(pltpu.VMEM(*shape) for shape in shapes),
        in_specs=[hbm] * 5,
        out_specs=(vmem,) * 4,
        scratch_shapes=[
            buf(ROWS, FEAT),
            buf(ROWS, FEAT),
            pltpu.SMEM((16,), jnp.int32),
            buf(BLOCK, FEAT, dtype=f32),
            buf(128, 384),
            buf(NY, NL, BLOCK, WA),
            buf(NY, NL, BLOCK, WB),
            buf(NY, NL, BLOCK, TAIL),
            buf(NY, NL, BLOCK, WA),
            buf(NY, NL, BLOCK, WB),
            buf(NY, NL, BLOCK, TAIL),
            buf(FEAT, 4 * HID),
            buf(2, 2 * HID, FEAT),
            buf(NY, 32, 3 * HID, dtype=f32),
            buf(NY, 32, 3 * HID),
            buf(2, 3, 32, 3 * HID),
            buf(NY, 32, 3 * HID),
            buf(NY, 32, 3 * HID),
            buf(NY, NL, BLOCK, RA),
            buf(NY, NL, BLOCK, RB),
            buf(NY - 1, NL, BLOCK, RA),
            buf(3, BLOCK, RA),
            buf(NL, BLOCK, RA),
            buf(3, NY, BLOCK, RB),
            buf(NY, BLOCK, RB),
            buf(NY - 1, BLOCK, RB),
            buf(NH, BLOCK, RA),
            buf(NH, BLOCK, RB),
            buf(2 * HID, 1024),
            pltpu.SemaphoreType.DMA((N_SEMS,)),
            pltpu.SemaphoreType.DMA((N_SEMS,)),
            pltpu.SemaphoreType.DMA((8,)),
        ],
        compiler_params=pltpu.CompilerParams(
            collective_id=0, has_side_effects=True, vmem_limit_bytes=44 * 1024 * 1024
        ),
    )(*arguments)
    return pl.pallas_call(
        write_out,
        out_shape=tuple(jax.ShapeDtypeStruct(*shape) for shape in shapes),
        in_specs=[vmem] * 4,
        out_specs=(hbm,) * 4,
        scratch_shapes=[pltpu.SemaphoreType.DMA((4,))],
        compiler_params=pltpu.CompilerParams(vmem_limit_bytes=4 * 1024 * 1024),
    )(*results)


def solution(mesh):
    return jax.shard_map(
        per_device,
        mesh=mesh,
        in_specs=(
            P("tok", "fin"),
            P("tok", "fin"),
            P(),
            P("fin", ("tok", "fout")),
            P(("tok", "fout"), "fin"),
        ),
        out_specs=(
            P("tok", "fin"),
            P("tok", "fin"),
            P("fin", ("tok", "fout")),
            P(("tok", "fout"), "fin"),
        ),
        check_vma=False,
    )
```

```python
import jax
import jax.numpy as jnp
from jax import lax
from jax.experimental import pallas as pl
from jax.experimental.pallas import tpu as pltpu
from jax.sharding import PartitionSpec as P

inv_root_two = 0.7071067811865476
inv_root_two_pi = 0.3989422804014327

NX, NY, NL, NH = 4, 8, 4, 3
NZ = NL * NH
ROWS = 6
BLOCK = 16
FEAT = 1536
HID = 128
LONGEST = 48
TAIL = FEAT // 4
FOLD = FEAT - TAIL
WA = 512
WB = FOLD - WA
WC = 256
RA = 384
RB = FOLD - RA
RC = 128
FAR = (4, 3, 5, 2, 6, 1, 7, 0)
N_SEMS = 80

bf16, f32 = jnp.bfloat16, jnp.float32


def place(d):
    return FAR.index(d % NY)


def sublane(v):
    return lax.broadcasted_iota(jnp.int32, v.shape, 1)


def fold(v):
    w = v.shape[2] // 4
    tail = v[:, :, 3 * w :]
    row = sublane(tail)
    segments = []
    for i in range(3):
        low = jnp.broadcast_to(tail[:, i : i + 1], tail.shape)
        high = jnp.broadcast_to(tail[:, 3 + i : 4 + i], tail.shape)
        main = v[:, :, i * w : (i + 1) * w]
        segments.append(jnp.where(row == 6, low, jnp.where(row == 7, high, main)))
    return jnp.concatenate(segments, axis=2)


def unfold(v):
    w = v.shape[2] // 3
    segments = [v[:, :, i * w : (i + 1) * w] for i in range(3)]
    row = sublane(segments[0])
    tail = jnp.zeros_like(segments[0])
    for i in range(6):
        source = segments[i % 3][:, 6 + i // 3 : 7 + i // 3]
        tail = jnp.where(row == i, jnp.broadcast_to(source, tail.shape), tail)
    real = [jnp.where(row < 6, segment, 0.0) for segment in segments]
    return jnp.concatenate(real + [tail], axis=2)


def kernel(
    tok_hbm, cot_hbm, len_hbm, w1_ref, w2_ref,
    out_ref, gtok_ref, g1v, g2v,
    tok_ref, cot_ref, len_ref, xb, pm,
    xa, xbk, xt, xsa, xsb, xst, wc, wt,
    rf, rs, rr, ag, ags,
    ysa, ysb, ray, rza, saz, rbz, sby, rby, vha, vhb,
    mt,
    send_sem, recv_sem, local_sem,
):
    t = lax.axis_index("tok")
    x = lax.axis_index("fin")
    f = lax.axis_index("fout")
    c = lax.rem(t, 2)
    y = lax.rem(lax.div(t, 2), NY)
    zl = lax.div(t, 2 * NY)
    z = f * NL + zl

    def on_y(d):
        return {"tok": (zl * NY + lax.rem(y + d + NY, NY)) * 2 + c}

    def on_z(d):
        far = lax.rem(z + d + NZ, NZ)
        return {
            "tok": (lax.rem(far, NL) * NY + y) * 2 + c,
            "fout": lax.div(far, NL),
        }

    def on_x(d):
        return {"fin": lax.rem(x + d, NX)}

    sibling = {"tok": t + 1 - 2 * c}

    sent = []

    def send(src, dst, device):
        i = len(sent)
        copy = pltpu.make_async_remote_copy(
            src_ref=src, dst_ref=dst,
            send_sem=send_sem.at[i], recv_sem=recv_sem.at[i],
            device_id=device, device_id_type=pl.DeviceIdType.MESH,
        )
        copy.start()
        sent.append(copy)
        return copy

    def arrived(copies):
        for copy in copies:
            copy.wait_recv()

    small = [
        pltpu.make_async_copy(src, dst, local_sem.at[4 + i])
        for i, (src, dst) in enumerate(
            ((len_hbm, len_ref), (cot_hbm, cot_ref), (tok_hbm, tok_ref))
        )
    ]
    for copy in small:
        copy.start()
    own_w1 = pltpu.make_async_copy(w1_ref, wc.at[:, 0:HID], local_sem.at[0])
    own_w2 = pltpu.make_async_copy(w2_ref, wt.at[0, 0:HID], local_sem.at[1])
    own_w1.start()
    own_w2.start()

    barrier = pltpu.get_barrier_semaphore()
    partners = (
        [sibling]
        + [on_x(d) for d in (1, 2, 3)]
        + [on_y(d) for d in (1, 2, 3, 4, 5, 6, 7)]
        + [on_z(d) for d in (1, -1, 2, -2, 4, -4)]
    )
    for device in partners:
        pl.semaphore_signal(
            barrier, inc=1, device_id=device, device_id_type=pl.DeviceIdType.MESH
        )

    for copy in small:
        copy.wait()
    position = t * ROWS + lax.broadcasted_iota(jnp.int32, (8, 128), 0)
    span = jnp.zeros((8, 128), jnp.int32)
    start = jnp.int32(0)
    for i in range(16):
        length = len_ref[i]
        end = start + length
        span = jnp.where((position >= start) & (position < end), length, span)
        start = end
    ratio = f32(LONGEST) / jnp.maximum(span, 1).astype(f32)
    scale = jnp.where(span > 0, jnp.sqrt(ratio), f32(0.0))
    scale = jnp.concatenate([scale] * (FEAT // 128), axis=1)[0:ROWS]
    xb[...] = jnp.zeros_like(xb)
    xb[0:ROWS] = tok_ref[...].astype(f32)
    xb[8 : 8 + ROWS] = cot_ref[...].astype(f32) * scale
    block = fold(xb[...].reshape(2, 8, FEAT)).reshape(BLOCK, FOLD).astype(bf16)
    home = place(0)
    xa[home, 0] = block[:, 0:WA]
    xbk[home, 0] = block[:, WA:]

    pl.semaphore_wait(barrier, len(partners))

    ga_z = [send(xa.at[home, 0], xa.at[home, -d % NL], on_z(d)) for d in (1, -1)]
    for d, cols in ((2, slice(0, WC)), (-2, slice(WC, WA))):
        ga_z.append(send(xa.at[home, 0, :, cols], xa.at[home, 2, :, cols], on_z(d)))
    gb_y = {
        place(-d): send(xbk.at[home, 0], xbk.at[place(-d), 0], on_y(d))
        for d in (2, 1, -1, -2, 4, 3, -3)
    }

    r = lax.broadcasted_iota(jnp.int32, (128, 384), 0)
    q = lax.broadcasted_iota(jnp.int32, (128, 384), 1)
    i = lax.rem(r, 8)
    late = jnp.where(i >= 3, 1, 0)
    spot = (i - 3 * late) * 128 + (r - i) + 6 + late
    pm[...] = jnp.where((i < 6) & (q == spot), f32(1.0), f32(0.0)).astype(bf16)
    own_w1.wait()
    own_w2.wait()
    wc[:, 2 * HID : 3 * HID] = wt[0, 0:HID].T
    wt[1, 0:HID] = wc[:, 0:HID].T

    arrived(ga_z)
    ga_y = {d: send(xa.at[home], xa.at[place(-d)], on_y(d)) for d in (2, -2, 1, -1)}
    sib_w1 = send(w1_ref, wc.at[:, HID : 2 * HID], sibling)
    sib_w2 = send(w2_ref, wt.at[0, HID : 2 * HID], sibling)
    gb_z = []
    for js, d in ((slice(4, 8), -2), (slice(0, 4), 2)):
        arrived([gb_y[j] for j in range(js.start, js.stop) if j != home])
        for to in (d, 1, -1):
            gb_z.append(send(xbk.at[js, 0], xbk.at[js, -to % NL], on_z(to)))
    ga_far = []
    for way, ks in ((1, slice(0, 2)), (-1, slice(2, 4))):
        arrived([ga_y[2 * way]])
        group = place(-2 * way)
        ga_far.append(
            send(xa.at[group, ks], xa.at[place(4), ks], on_y(2 * way))
        )
        ga_far.append(send(xa.at[group], xa.at[place(-3 * way)], on_y(way)))
    arrived([sib_w1, sib_w2])
    wc[:, 3 * HID : 4 * HID] = wt[0, HID : 2 * HID].T
    wt[1, HID : 2 * HID] = wc[:, HID : 2 * HID].T
    arrived([ga_y[1], ga_y[-1]] + ga_far)
    arrived(gb_z)

    def tails(dst, part_a, part_b, g):
        js = slice(2 * g, 2 * g + 2)
        whole = jnp.concatenate(
            [part_a[js].reshape(128, WA), part_b[js].reshape(128, WB)], axis=1
        )
        stacked = jnp.concatenate(
            [whole[:, i * TAIL : (i + 1) * TAIL] for i in range(3)], axis=0
        )
        value = jnp.dot(pm[...], stacked, preferred_element_type=f32)
        dst[js] = value.astype(bf16).reshape(2, NL, BLOCK, TAIL)

    def partial(h):
        tails(xt, xa, xbk, 2 * h)
        tails(xt, xa, xbk, 2 * h + 1)
        js = slice(4 * h, 4 * h + 4)
        lhs = jnp.concatenate(
            [
                xa[js].reshape(256, WA),
                xbk[js].reshape(256, WB),
                xt[js].reshape(256, TAIL),
            ],
            axis=1,
        )
        pre = jnp.dot(lhs, wc[:, 0 : 2 * HID], preferred_element_type=f32)
        back = jnp.dot(lhs, wc[:, 2 * HID : 4 * HID], preferred_element_type=f32)
        pre = pre.reshape(16, 2, 8, 2 * HID)[:, 0]
        back = back.reshape(16, 2, 8, 2 * HID)[:, 1]
        value = fold(jnp.concatenate([pre, back], axis=2)).reshape(4, 32, 3 * HID)
        rf[js] = value
        rs[js] = value.astype(bf16)

    x_in = {}
    for h in range(2):
        partial(h)
        x_in[h] = []
        for d in (2, 1, 3):
            j = 4 * h + lax.rem(x + d, NX)
            x_in[h].append(send(rs.at[j], rr.at[h, d - 1], on_x(d)))
    x_out = {}
    for h in range(2):
        arrived(x_in[h])
        mine = 4 * h + x
        total = rf[mine]
        for d in range(3):
            total = total + rr[h, d].astype(f32)
        total = unfold(total.reshape(4, 8, 3 * HID))
        pre, back = total[:, :, 0 : 2 * HID], total[:, :, 2 * HID : 4 * HID]
        cdf = 0.5 * (1.0 + lax.erf(pre * inv_root_two))
        density = jnp.exp(-0.5 * pre * pre) * inv_root_two_pi
        act = pre * cdf
        gp = back * (cdf + pre * density)
        value = jnp.concatenate(
            [act[:, :, 0:HID], gp[:, :, 0:HID], act[:, :, HID:], gp[:, :, HID:]],
            axis=2,
        )
        ag[mine] = fold(value).reshape(32, 3 * HID).astype(bf16)
        x_out[h] = [send(ag.at[mine], ag.at[mine], on_x(d)) for d in (2, 1, 3)]

    xs = [send(xa, xsa, sibling), send(xbk, xsb, sibling)]

    def outputs(h):
        js = slice(4 * h, 4 * h + 4)
        u = unfold(ag[js].astype(f32).reshape(16, 8, 3 * HID)).reshape(128, 4 * HID)
        u = u.astype(bf16)
        act2 = jnp.concatenate([u[:, 0:HID], u[:, 2 * HID : 3 * HID]], axis=1)
        gp2 = jnp.concatenate([u[:, HID : 2 * HID], u[:, 3 * HID :]], axis=1)
        fwd = jnp.dot(act2, wt[0], preferred_element_type=f32)
        bwd = jnp.dot(gp2, wt[1], preferred_element_type=f32)
        fwd = fold(fwd.reshape(16, 8, FEAT))
        bwd = fold(bwd.reshape(16, 8, FEAT))
        value = jnp.concatenate([fwd, bwd], axis=1).astype(bf16)
        ysa[js] = value[:, :, 0:RA].reshape(4, NL, BLOCK, RA)
        ysb[js] = value[:, :, RA:].reshape(4, NL, BLOCK, RB)

    ra_y, rb_z = [], ([], [])
    for h in range(2):
        arrived(x_out[h])
        outputs(h)
        js = slice(4 * h, 4 * h + 4)
        for j in range(4 * h, min(4 * h + 4, NY - 1)):
            ra_y.append(send(ysa.at[j], ray.at[j], on_y(FAR[j])))
        d = (2, -2)[h]
        rb_z[h].append(send(ysb.at[js, 2], rbz.at[2, js], on_z(d)))
        for w, d in enumerate((1, -1)):
            rb_z[h].append(send(ysb.at[js, d % NL], rbz.at[w, js], on_z(d)))

    ag_sib = send(ag, ags, sibling)

    def spread(v, lanes):
        v = unfold(v.astype(f32).reshape(32, 8, 3 * HID))[:, :, lanes]
        none = jnp.zeros((32, 8, HID), f32)
        first = jnp.concatenate([v[:, :, HID:], none], axis=2)
        second = jnp.concatenate([none, v[:, :, 0:HID]], axis=2)
        both = jnp.concatenate([first, second], axis=1)
        return both.reshape(512, 2 * HID).astype(bf16)

    def part_b_y(h):
        arrived(rb_z[h])
        js = slice(4 * h, 4 * h + 4)
        value = ysb[js, 0].astype(f32)
        for w in range(3):
            value = value + rbz[w, js].astype(f32)
        sby[js] = value.astype(bf16)
        return [
            send(sby.at[j], rby.at[j], on_y(FAR[j]))
            for j in range(4 * h, min(4 * h + 4, NY - 1))
        ]

    rb_y = part_b_y(0)
    rb_y += part_b_y(1)
    mt[:, 0:512] = spread(ag[...], slice(0, 2 * HID)).T

    def weight_grads(src, src_sib, width, first):
        for n in range(0, width, 256):
            lanes = slice(n, min(n + 256, width))
            size = lanes.stop - lanes.start
            lhs = src[:, :, :, lanes].reshape(512, size)
            rhs = src_sib[:, :, :, lanes].reshape(512, size)
            g = jnp.dot(mt[:, 0:512], lhs, preferred_element_type=f32)
            g = g + jnp.dot(mt[:, 512:1024], rhs, preferred_element_type=f32)
            cols = slice(first + n, first + n + size)
            g1v[cols, :] = g[0:HID].T
            g2v[:, cols] = g[HID:]


    arrived(xs)
    for g in range(4):
        tails(xst, xsa, xsb, g)
    arrived([ag_sib])
    mt[:, 512:1024] = spread(ags[...], slice(2 * HID, 4 * HID)).T

    arrived(ra_y)
    value = ysa[home].astype(f32)
    for j in range(NY - 1):
        value = value + ray[j].astype(f32)
    saz[...] = value.astype(bf16)
    ra_z = [send(saz.at[d % NL], rza.at[w], on_z(d)) for w, d in enumerate((1, -1))]
    for d, cols in ((2, slice(0, RC)), (-2, slice(RC, RA))):
        ra_z.append(send(saz.at[2, :, cols], rza.at[2, :, cols], on_z(d)))
    weight_grads(xt, xst, TAIL, FOLD)

    arrived(ra_z)
    value = saz[0].astype(f32)
    for w in range(3):
        value = value + rza[w].astype(f32)
    vha[f] = value.astype(bf16)
    last = [send(vha.at[f], vha.at[f], on_z(d)) for d in (4, -4)]
    arrived(rb_y)
    value = sby[home].astype(f32)
    for j in range(NY - 1):
        value = value + rby[j].astype(f32)
    vhb[f] = value.astype(bf16)
    last += [send(vhb.at[f], vhb.at[f], on_z(d)) for d in (4, -4)]
    weight_grads(xa, xsa, WA, 0)
    weight_grads(xbk, xsb, WB, WA)
    arrived(last)
    value = jnp.concatenate(
        [
            v[0].astype(f32) + v[1].astype(f32) + v[2].astype(f32)
            for v in (vha, vhb)
        ],
        axis=1,
    )
    value = unfold(value.reshape(2, 8, FOLD))
    out_ref[...] = value[0, 0:ROWS].astype(bf16)
    gtok_ref[...] = value[1, 0:ROWS].astype(bf16)

    for copy in sent:
        copy.wait_send()


def write_out(*refs):
    sem = refs[8]
    copies = [pltpu.make_async_copy(refs[i], refs[4 + i], sem.at[i]) for i in range(4)]
    for copy in copies:
        copy.start()
    for copy in copies:
        copy.wait()


def per_device(tokens, cotangent, image_lengths, fc1_weight, fc2_weight):
    vmem = pl.BlockSpec(memory_space=pltpu.VMEM)
    hbm = pl.BlockSpec(memory_space=pl.ANY)

    def buf(*shape, dtype=bf16):
        return pltpu.VMEM(shape, dtype)

    shapes = (
        ((ROWS, FEAT), bf16),
        ((ROWS, FEAT), bf16),
        ((FEAT, HID), f32),
        ((HID, FEAT), f32),
    )
    arguments = [
        pltpu.with_memory_space_constraint(a, pltpu.HBM)
        for a in (tokens, cotangent, image_lengths, fc1_weight, fc2_weight)
    ]
    results = pl.pallas_call(
        kernel,
        out_shape=tuple(pltpu.VMEM(*shape) for shape in shapes),
        in_specs=[hbm] * 5,
        out_specs=(vmem,) * 4,
        scratch_shapes=[
            buf(ROWS, FEAT),
            buf(ROWS, FEAT),
            pltpu.SMEM((16,), jnp.int32),
            buf(BLOCK, FEAT, dtype=f32),
            buf(128, 384),
            buf(NY, NL, BLOCK, WA),
            buf(NY, NL, BLOCK, WB),
            buf(NY, NL, BLOCK, TAIL),
            buf(NY, NL, BLOCK, WA),
            buf(NY, NL, BLOCK, WB),
            buf(NY, NL, BLOCK, TAIL),
            buf(FEAT, 4 * HID),
            buf(2, 2 * HID, FEAT),
            buf(NY, 32, 3 * HID, dtype=f32),
            buf(NY, 32, 3 * HID),
            buf(2, 3, 32, 3 * HID),
            buf(NY, 32, 3 * HID),
            buf(NY, 32, 3 * HID),
            buf(NY, NL, BLOCK, RA),
            buf(NY, NL, BLOCK, RB),
            buf(NY - 1, NL, BLOCK, RA),
            buf(3, BLOCK, RA),
            buf(NL, BLOCK, RA),
            buf(3, NY, BLOCK, RB),
            buf(NY, BLOCK, RB),
            buf(NY - 1, BLOCK, RB),
            buf(NH, BLOCK, RA),
            buf(NH, BLOCK, RB),
            buf(2 * HID, 1024),
            pltpu.SemaphoreType.DMA((N_SEMS,)),
            pltpu.SemaphoreType.DMA((N_SEMS,)),
            pltpu.SemaphoreType.DMA((8,)),
        ],
        compiler_params=pltpu.CompilerParams(
            collective_id=0, has_side_effects=True, vmem_limit_bytes=44 * 1024 * 1024
        ),
    )(*arguments)
    return pl.pallas_call(
        write_out,
        out_shape=tuple(jax.ShapeDtypeStruct(*shape) for shape in shapes),
        in_specs=[vmem] * 4,
        out_specs=(hbm,) * 4,
        scratch_shapes=[pltpu.SemaphoreType.DMA((4,))],
        compiler_params=pltpu.CompilerParams(vmem_limit_bytes=4 * 1024 * 1024),
    )(*results)


def solution(mesh):
    return jax.shard_map(
        per_device,
        mesh=mesh,
        in_specs=(
            P("tok", "fin"),
            P("tok", "fin"),
            P(),
            P("fin", ("tok", "fout")),
            P(("tok", "fout"), "fin"),
        ),
        out_specs=(
            P("tok", "fin"),
            P("tok", "fin"),
            P("fin", ("tok", "fout")),
            P(("tok", "fout"), "fin"),
        ),
        check_vma=False,
    )
```
